128 devices in a mesh: sx: 16 (over x, z_lo, core), sy: 8 (over y, z_hi).
Axes of the slice: x: 4, y: 4, z: 4 (z_hi: 2, z_lo: 2; z = z_hi * 2 + z_lo), core: 2. Of those that a mesh axis runs over, the one named last changes fastest.
Arguments:
- volume: bfloat16 [64, 64, 256, 64], P('sx', 'sy'), may hold values from -6 to 6
- first_kernel: bfloat16 [3, 3, 3, 64, 128], replicated, may hold values from -0.15625 to 0.15625
- second_kernel: bfloat16 [3, 3, 3, 128, 128], P(None, None, None, None, 'sx'), may hold values from -0.109375 to 0.109375
- third_kernel: bfloat16 [3, 3, 3, 128, 128], P(None, None, None, 'sx'), may hold values from -0.109375 to 0.109375
- cotangent: bfloat16 [32, 32, 128, 128], P('sy', None, None, 'sx'), may hold values from -0.119628906 to 0.119628906
Outputs:
- output: bfloat16 [32, 32, 128, 128], P('sy', None, None, 'sx')
- first_grad: float32 [3, 3, 3, 64, 128], replicated
- second_grad: float32 [3, 3, 3, 128, 128], P(None, None, None, None, 'sx')
- third_grad: float32 [3, 3, 3, 128, 128], P(None, None, None, 'sx')
The draws below stay inside these ranges and needn't reach their ends.
All inputs are finite; a program needn't handle non-finite values.
Results may differ from the reference program's by a relative error of at most 0.034.
The reference program's roundings to bfloat16 on the way (of `pooled`, `hidden`, `second_pre_grad`, `pooled_grad` and `first_pre_grad`) count: a program that leaves them out, or rounds other values in their place, can miss the bound.
Values may be sent and summed in bfloat16 or wider, within the bound.
No kernel may reach another device: no remote copies, remote signals or barrier semaphores. Data moves between devices by JAX's collectives and lax.ppermute only.
A program may use at most 192 MiB of HBM per device.

```python
import jax
import jax.numpy as jnp
from jax import lax

WW = 256
CI = 64
C = 128
DEPTH = 64
HEIGHT = 64
PD = 32
PH = 32
PW = 128


def block_levels(stream_key, extent, split, least, high):
    factor_of, own = 1.0, jax.random.fold_in(stream_key, 6)
    for position, blocks in split:
        steps = jnp.exp(jax.random.uniform(jax.random.fold_in(own, position), (blocks,), jnp.float32, least / len(split), high / len(split)))
        factor_of = factor_of * jnp.repeat(steps, extent[position] // blocks).reshape([-1 if axis == position else 1 for axis in range(len(extent))])
    return factor_of


def noise(rng, dims, width, reach, split=(), kind=jnp.bfloat16):
    level = block_levels(rng, dims, split, -0.22, 0.18) if split else 1.0
    result = jax.random.normal(rng, dims, jnp.float32) * width * level
    return jnp.minimum(jnp.maximum(result, -reach), reach).astype(kind)


def setup_inputs(seed: int = 0) -> dict:
    seeds = jax.random.split(jax.random.key(seed), 6)
    volume = noise(seeds[0], (DEPTH, HEIGHT, WW, CI), 1.0, 6.0, ((0, 16), (1, 8)))
    first_kernel = noise(seeds[1], (3, 3, 3, CI, C), (27 * CI) ** -0.5, 0.15625)
    second_kernel = noise(seeds[2], (3, 3, 3, C, C), (27 * C) ** -0.5, 0.109375, ((4, 16),))
    third_kernel = noise(seeds[3], (3, 3, 3, C, C), (27 * C) ** -0.5, 0.109375, ((3, 16),))
    cotangent = noise(seeds[4], (PD, PH, PW, C), 0.02, 0.119628906, ((0, 8), (3, 16)))
    return dict(volume=volume, first_kernel=first_kernel, second_kernel=second_kernel, third_kernel=third_kernel, cotangent=cotangent)


leak_slope = 0.2

def conv_valid(padded, kernel):
    return lax.conv_general_dilated(padded.astype(jnp.float32)[None], kernel.astype(jnp.float32), (1, 1, 1), 'VALID', dimension_numbers=('NDHWC', 'DHWIO', 'NDHWC'), precision=lax.Precision.HIGHEST)[0]

def pad_all(values):
    return jnp.pad(values, ((1, 1), (1, 1), (1, 1), (0, 0)))

def flipped(kernel):
    return jnp.swapaxes(kernel[::-1, ::-1, ::-1], 3, 4)

def kernel_grad(padded, cotangent):
    depth_cells, height_cells, width_cells, out_width = cotangent.shape
    inner_width = padded.shape[3]
    flat_cot = cotangent.astype(jnp.float32).reshape(-1, out_width)
    tap_list = []
    for a in range(3):
        for b in range(3):
            for c in range(3):
                window = padded[a:a + depth_cells, b:b + height_cells, c:c + width_cells].astype(jnp.float32).reshape(-1, inner_width)
                tap_list.append(lax.dot_general(window, flat_cot, (((0,), (0,)), ((), ())), precision=lax.Precision.HIGHEST))
    return jnp.stack(tap_list).reshape(3, 3, 3, inner_width, out_width)

def leaky_relu(values):
    return jnp.where(values > 0, values, leak_slope * values)

def leaky_slope(values):
    return jnp.where(values > 0, 1.0, leak_slope)

def reference(volume, first_kernel, second_kernel, third_kernel, cotangent):
    first_pre = conv_valid(pad_all(volume), first_kernel)
    depth_cells, height_cells, width_cells, channels = first_pre.shape
    pooled = leaky_relu(first_pre).reshape(depth_cells // 2, 2, height_cells // 2, 2, width_cells // 2, 2, channels).mean(axis=(1, 3, 5)).astype(jnp.bfloat16)
    second_pre = conv_valid(pad_all(pooled), second_kernel)
    hidden = leaky_relu(second_pre).astype(jnp.bfloat16)
    output = conv_valid(pad_all(hidden), third_kernel).astype(jnp.bfloat16)
    hidden_grad = conv_valid(pad_all(cotangent), flipped(third_kernel))
    third_grad = kernel_grad(pad_all(hidden), cotangent)
    second_pre_grad = (hidden_grad * leaky_slope(second_pre)).astype(jnp.bfloat16)
    second_grad = kernel_grad(pad_all(pooled), second_pre_grad)
    pooled_grad = conv_valid(pad_all(second_pre_grad), flipped(second_kernel)).astype(jnp.bfloat16)
    spread = jnp.repeat(jnp.repeat(jnp.repeat(pooled_grad.astype(jnp.float32), 2, 0), 2, 1), 2, 2) / 8.0
    first_pre_grad = (spread * leaky_slope(first_pre)).astype(jnp.bfloat16)
    first_grad = kernel_grad(pad_all(volume), first_pre_grad)
    return (output, first_grad, second_grad, third_grad)
```

```python
import jax
import jax.numpy as jnp
from jax import lax
from jax.sharding import PartitionSpec as P

leak_slope = 0.2


def padded_2(cells, sides, width):
    for axis, dim in sides:
        count = lax.axis_size(axis)
        ends = count - 1
        head = lax.slice_in_dim(cells, 0, width, axis=dim)
        tail = lax.slice_in_dim(cells, cells.shape[dim] - width, cells.shape[dim], axis=dim)
        cells = jnp.concatenate(
            [
                lax.ppermute(tail, axis, [(i, (i + 1) % count) for i in range(ends)]),
                cells,
                lax.ppermute(head, axis, [((i + 1) % count, i) for i in range(ends)]),
            ],
            axis=dim,
        )
    return cells


def conv_valid(padded, kernel):
    return lax.conv_general_dilated(
        padded[None],
        kernel,
        (1, 1, 1),
        "VALID",
        dimension_numbers=("NDHWC", "DHWIO", "NDHWC"),
        preferred_element_type=jnp.float32,
    )[0]


def flipped(kernel):
    return jnp.swapaxes(kernel[::-1, ::-1, ::-1], 3, 4)


def kernel_grad(padded, cotangent):
    depth_cells, height_cells, width_cells, out_width = cotangent.shape
    inner_width = padded.shape[3]
    flat_cot = cotangent.reshape(-1, out_width)
    tap_list = []
    for a in range(3):
        for b in range(3):
            for c in range(3):
                window = padded[
                    a : a + depth_cells, b : b + height_cells, c : c + width_cells
                ].reshape(-1, inner_width)
                tap_list.append(
                    lax.dot_general(
                        window,
                        flat_cot,
                        (((0,), (0,)), ((), ())),
                        preferred_element_type=jnp.float32,
                    )
                )
    return jnp.stack(tap_list).reshape(3, 3, 3, inner_width, out_width)


def leaky_relu(values):
    return jnp.where(values > 0, values, leak_slope * values)


def leaky_slope(values):
    return jnp.where(values > 0, 1.0, leak_slope)


def pad_width(values):
    return jnp.pad(values, ((0, 0), (0, 0), (1, 1), (0, 0)))


def swap_places(ways):
    return [
        (a * 8 + b, (2 * b + a % 2) * 8 + a // 2)
        if ways > 0
        else ((2 * b + a % 2) * 8 + a // 2, a * 8 + b)
        for a in range(16)
        for b in range(8)
    ]


def to_channels(values):
    moved = lax.ppermute(jnp.swapaxes(values, 2, 3), ("sx", "sy"), swap_places(1))
    parts = jnp.swapaxes(moved.reshape(8, 16, 8, 128), 0, 1)
    parts = lax.all_to_all(parts, "sx", 0, 0, tiled=True)
    parts = parts.reshape(8, 2, 2, 4, 8, 128).transpose(1, 2, 0, 3, 4, 5)
    return jnp.swapaxes(parts.reshape(4, 32, 8, 128), 2, 3)


def to_space(values):
    parts = jnp.swapaxes(values, 2, 3).reshape(2, 2, 8, 4, 8, 128)
    parts = parts.transpose(2, 0, 1, 3, 4, 5).reshape(16, 8, 8, 128)
    parts = lax.all_to_all(parts, "sx", 0, 0, tiled=True)
    cells = jnp.swapaxes(parts, 0, 1).reshape(2, 4, 128, 128)
    return jnp.swapaxes(lax.ppermute(cells, ("sx", "sy"), swap_places(-1)), 2, 3)


def sum_parts(parts, axis):
    got = lax.all_to_all(parts.astype(jnp.bfloat16), axis, 0, 0, tiled=True)
    return got.astype(jnp.float32).sum(0)


def spread_part(part, axis, count):
    part = part.astype(jnp.bfloat16)
    got = lax.all_to_all(
        jnp.broadcast_to(part[None], (count,) + part.shape), axis, 0, 0, tiled=True
    )
    return got.reshape((-1,) + part.shape[1:])


def mid_faces(values):
    return pad_width(padded_2(values, (("sx", 0), ("sy", 1)), 1))


def on_device(volume, first_kernel, second_kernel, third_kernel, cotangent):
    volume_pad = pad_width(padded_2(volume, (("sx", 0), ("sy", 1)), 1))
    first_pre = conv_valid(volume_pad, first_kernel)
    depth_cells, height_cells, width_cells, channels = first_pre.shape
    pooled = (
        leaky_relu(first_pre)
        .reshape(depth_cells // 2, 2, height_cells // 2, 2, width_cells // 2, 2, channels)
        .mean(axis=(1, 3, 5))
        .astype(jnp.bfloat16)
    )
    shares = jnp.concatenate(
        [
            jnp.swapaxes(second_kernel, 3, 4).reshape(216, 128),
            third_kernel.reshape(216, 128),
        ]
    )
    filters = lax.all_gather(shares, "sx", axis=0, tiled=True).reshape(16, 2, 27, 8, 128)
    filters = filters.transpose(1, 2, 0, 3, 4).reshape(2, 3, 3, 3, 128, 128)
    second_full = jnp.swapaxes(filters[0], 3, 4)
    third_full = filters[1]
    pooled_pad = mid_faces(pooled)
    second_pre = conv_valid(pooled_pad, second_full)
    hidden = leaky_relu(second_pre).astype(jnp.bfloat16)
    hidden_pad = mid_faces(hidden)
    output = to_channels(conv_valid(hidden_pad, third_full).astype(jnp.bfloat16))
    cot_space = to_space(cotangent)
    hidden_grad = conv_valid(mid_faces(cot_space), flipped(third_full))
    third_whole = kernel_grad(hidden_pad, cot_space)
    second_pre_grad = (hidden_grad * leaky_slope(second_pre)).astype(jnp.bfloat16)
    second_whole = kernel_grad(pooled_pad, second_pre_grad)
    pooled_grad = conv_valid(mid_faces(second_pre_grad), flipped(second_full)).astype(jnp.bfloat16)
    grads = jnp.stack([jnp.swapaxes(second_whole, 3, 4), third_whole]).astype(jnp.bfloat16)
    grads = grads.reshape(54, 16, 8, 128).swapaxes(0, 1).reshape(16, 432, 128)
    share = sum_parts(grads, "sx")
    share = sum_parts(jnp.pad(share, ((0, 80), (0, 0))).reshape(8, 64, 128), "sy")
    share = spread_part(share, "sy", 8)[:432].astype(jnp.float32).reshape(2, 3, 3, 3, 8, 128)
    second_grad, third_grad = jnp.swapaxes(share[0], 3, 4), share[1]
    spread = (
        jnp.broadcast_to(
            pooled_grad.astype(jnp.float32)[:, None, :, None, :, None, :],
            (depth_cells // 2, 2, height_cells // 2, 2, width_cells // 2, 2, channels),
        ).reshape(depth_cells, height_cells, width_cells, channels)
        / 8.0
    )
    first_pre_grad = (spread * leaky_slope(first_pre)).astype(jnp.bfloat16)
    first_part = kernel_grad(volume_pad, first_pre_grad).reshape(1728, 128)
    first_part = jnp.pad(first_part, ((0, 320), (0, 0))).reshape(128, 16, 128)
    first_sum = spread_part(sum_parts(first_part, ("sx", "sy")), ("sx", "sy"), 128)
    first_grad = first_sum[:1728].astype(jnp.float32).reshape(3, 3, 3, 64, 128)
    return (output, first_grad, second_grad, third_grad)


def solution(mesh):
    in_specs = (
        P("sx", "sy", None, None),
        P(),
        P(None, None, None, None, "sx"),
        P(None, None, None, "sx", None),
        P("sy", None, None, "sx"),
    )
    out_specs = (
        P("sy", None, None, "sx"),
        P(),
        P(None, None, None, None, "sx"),
        P(None, None, None, "sx", None),
    )
    return jax.shard_map(
        on_device, mesh=mesh, in_specs=in_specs, out_specs=out_specs, check_vma=False
    )
```

```python
import jax
import jax.numpy as jnp
import numpy as np
from jax import lax
from jax.experimental import pallas as pl
from jax.experimental.pallas import tpu as pltpu
from jax.sharding import PartitionSpec as P

leak_slope = 0.2
both = ("sx", "sy")
vmem_bytes = 56 * 1024 * 1024


def swap_places(ways):
    pairs = [(a * 8 + b, (2 * b + a % 2) * 8 + a // 2) for a in range(16) for b in range(8)]
    return pairs if ways > 0 else [(there, here) for here, there in pairs]


def neighbours(first, last, axis):
    ends = lax.axis_size(axis) - 1
    return (
        lax.ppermute(last, axis, [(i, i + 1) for i in range(ends)]),
        lax.ppermute(first, axis, [(i + 1, i) for i in range(ends)]),
    )


def sum_parts(parts, axis):
    got = lax.all_to_all(parts.astype(jnp.bfloat16), axis, 0, 0, tiled=True)
    return got.astype(jnp.float32).sum(0)


def spread_part(part, axis, count):
    part = part.astype(jnp.bfloat16)
    got = lax.all_to_all(
        jnp.broadcast_to(part[None], (count,) + part.shape), axis, 0, 0, tiled=True
    )
    return got.reshape((-1,) + part.shape[1:])


def dot(left, right):
    return jnp.dot(left, right, preferred_element_type=jnp.float32)


def row_before(values):
    rows = lax.broadcasted_iota(jnp.int32, values.shape, 0)
    return jnp.where(rows == 0, 0.0, pltpu.roll(values, 1, 0))


def row_after(values):
    count = values.shape[0]
    rows = lax.broadcasted_iota(jnp.int32, values.shape, 0)
    return jnp.where(rows == count - 1, 0.0, pltpu.roll(values, count - 1, 0))


def call(body, outs, scratch, operands, smem=0, flops=0, name=None):
    size = sum(int(np.prod(a.shape)) * a.dtype.itemsize for a in operands)
    size += sum(int(np.prod(shape)) * jnp.dtype(kind).itemsize for shape, kind in outs)
    whole = pl.BlockSpec(memory_space=pltpu.VMEM)
    specs = [whole] * (len(operands) - smem) + [pl.BlockSpec(memory_space=pltpu.SMEM)] * smem
    return pl.pallas_call(
        body,
        out_shape=[jax.ShapeDtypeStruct(shape, kind) for shape, kind in outs],
        in_specs=specs,
        out_specs=[whole] * len(outs),
        scratch_shapes=[pltpu.VMEM(shape, kind) for shape, kind in scratch],
        compiler_params=pltpu.CompilerParams(vmem_limit_bytes=vmem_bytes),
        cost_estimate=pl.CostEstimate(flops=flops, bytes_accessed=size, transcendentals=0),
        name=name,
    )(*operands)


def pair_select():
    sel = np.zeros((256, 4, 128), np.float32)
    for k, offset in enumerate((0, 1, -1, 2)):
        for p in range(128):
            if 0 <= 2 * p + offset < 256:
                sel[2 * p + offset, k, p] = 1
    return jnp.asarray(sel.reshape(256, 512), jnp.bfloat16)


def pair_filters(kernel):
    taps = kernel.reshape(9, 3, 64, 128)
    none = jnp.zeros((9, 64, 128), kernel.dtype)
    even = jnp.concatenate([taps[:, 1], taps[:, 2], taps[:, 0], none], axis=1)
    odd = jnp.concatenate([taps[:, 0], taps[:, 1], none, taps[:, 2]], axis=1)
    return jnp.concatenate([even, odd], axis=2)


def first_body(vc, vzl, vzh, vyl, vyh, w1, sel, pooled, bits, xt, xc, acc):
    for z in range(6):
        rows = vzl[0] if z == 0 else vzh[0] if z == 5 else vc[z - 1]
        got = dot(rows.reshape(512, 256), sel[...]).astype(jnp.bfloat16)
        low = dot(vyl[z, 0], sel[...]).astype(jnp.bfloat16)
        high = dot(vyh[z, 0], sel[...]).astype(jnp.bfloat16)
        for k in range(4):
            lanes = slice(k * 128, k * 128 + 128)
            place = slice(k * 64, k * 64 + 64)
            xt[z, place, 0:128] = low[:, lanes]
            xt[z, place, 1152:1280] = high[:, lanes]
            for y in range(8):
                xt[z, place, (y + 1) * 128 : (y + 2) * 128] = got[y * 64 : y * 64 + 64, lanes]
        xc[z] = xt[z].T

    @pl.loop(0, 2)
    def _(zp):
        for zz in range(2):
            total = None
            for a in range(3):
                for b in range(3):
                    part = dot(xc[2 * zp + zz + a, b * 128 : b * 128 + 1024, :], w1[3 * a + b])
                    total = part if total is None else total + part
            acc[zz] = total
        for yp in range(4):
            mean = jnp.zeros((128, 128), jnp.float32)
            mask = jnp.zeros((128, 128), jnp.int32)
            for zz in range(2):
                for yy in range(2):
                    for par in range(2):
                        row = (2 * yp + yy) * 128
                        v = acc[zz, row : row + 128, par * 128 : par * 128 + 128]
                        up = v > 0
                        mean += jnp.where(up, v, leak_slope * v)
                        mask |= jnp.where(up, 1 << (zz * 4 + yy * 2 + par), 0)
            pooled[zp, yp] = (mean * 0.125).astype(jnp.bfloat16)
            bits[zp, yp] = mask


def first_section(vc, vzl, vzh, vyl, vyh, w1):
    return call(
        first_body,
        [
            ((2, 4, 128, 128), jnp.bfloat16),
            ((2, 4, 128, 128), jnp.int32),
            ((6, 256, 1280), jnp.bfloat16),
        ],
        [((6, 1280, 256), jnp.bfloat16), ((2, 1024, 256), jnp.float32)],
        [vc, vzl, vzh, vyl, vyh, w1, pair_select()],
        flops=5_000_000_000,
        name="first",
    )


def lay_filters(place, tap_of, turn):
    for b in range(3):
        for four in range(4):
            for c in range(3):
                for two in range(2):
                    a = four - two
                    lanes = slice(c * 256 + two * 128, c * 256 + two * 128 + 128)
                    block = (b, slice(four * 128, four * 128 + 128), lanes)
                    if 0 <= a < 3:
                        tap = tap_of(a, b, c)
                        place[block] = tap.T if turn else tap
                    else:
                        place[block] = jnp.zeros((128, 128), jnp.bfloat16)


def conv_rows(source, lanes, filters, total, count):
    rows = count * 128
    parts = None
    for b in range(3):
        part = dot(source[b : b + count, :, lanes].reshape(rows, 512), filters[b])
        parts = part if parts is None else parts + part
    total[0:rows, :] = parts


def joined(total, y):
    rows = slice(y * 128, y * 128 + 128)
    return (
        row_before(total[rows, 0:256]) + total[rows, 256:512] + row_after(total[rows, 512:768])
    )


def cot_body(cc, cl, ch, k3, hidden_grad, cot3, cells, filters, total):
    for z in range(6):
        part = (cl, cc, ch)[z // 2]
        for y in range(8):
            cells[y, :, z * 128 : z * 128 + 128] = part[z % 2, y].T
    lay_filters(filters, lambda a, b, c: k3[(2 - a) * 9 + (2 - b) * 3 + 2 - c], True)
    for j in range(2):
        conv_rows(cells, slice(j * 256, j * 256 + 512), filters, total, 6)
        for y in range(6):
            hidden_grad[y, :, j * 256 : j * 256 + 256] = joined(total, y)
    for y in range(4):
        own = cells[y + 2, :, 256:512].astype(jnp.float32)
        rows = slice(y * 128, y * 128 + 128)
        cot3[rows, 0:256] = row_after(own).astype(jnp.bfloat16)
        cot3[rows, 256:512] = own.astype(jnp.bfloat16)
        cot3[rows, 512:768] = row_before(own).astype(jnp.bfloat16)


def cot_section(cc, cl, ch, k3):
    return call(
        cot_body,
        [((6, 128, 512), jnp.float32), ((512, 768), jnp.bfloat16)],
        [
            ((8, 128, 768), jnp.bfloat16),
            ((3, 512, 768), jnp.bfloat16),
            ((768, 768), jnp.float32),
        ],
        [cc, cl, ch, k3],
        flops=3_600_000_000,
        name="cot",
    )


def grad_taps(turned, cot3, store):
    for b in range(3):
        full = dot(turned[:, b * 128 : b * 128 + 512], cot3[...])
        for a in range(3):
            for c in range(3):
                low = full[a * 128 : a * 128 + 128, c * 256 : c * 256 + 128]
                high = full[a * 128 + 128 : a * 128 + 256, c * 256 + 128 : c * 256 + 256]
                store(9 * a + 3 * b + c, (low + high).astype(jnp.bfloat16))


def mid_body(
    pc, pzl, pzh, pyl, pyh, hidden_grad, cot3, k2, k3, flags,
    output, grads, spg, cells, hidden, filters, total, spg3, turned,
):
    for z in range(6):
        lanes = slice(z * 128, z * 128 + 128)
        part = (pzl, pc, pzh)[z // 2]
        for y in range(2):
            cells[y, :, lanes] = pyl[z, y]
            cells[y + 6, :, lanes] = pyh[z, y]
        for y in range(4):
            cells[y + 2, :, lanes] = part[z % 2, y]
    lay_filters(filters, lambda a, b, c: k2[9 * a + 3 * b + c], True)
    lane = lax.broadcasted_iota(jnp.int32, (128, 256), 1)
    for j in range(2):
        conv_rows(cells, slice(j * 256, j * 256 + 512), filters, total, 6)
        edge = lane < 128 if j == 0 else lane >= 128
        inside = jnp.where(edge, flags[j], 1.0)
        for y in range(6):
            pre = joined(total, y)
            keep = inside * flags[2] if y == 0 else inside * flags[3] if y == 5 else inside
            lanes = slice(j * 256, j * 256 + 256)
            up = pre > 0
            hidden[y, :, lanes] = (jnp.where(up, pre, leak_slope * pre) * keep).astype(
                jnp.bfloat16
            )
            back = hidden_grad[y, :, lanes]
            spg[y, :, lanes] = (jnp.where(up, back, leak_slope * back) * keep).astype(
                jnp.bfloat16
            )
    turned[...] = hidden[...].reshape(768, 512).T

    def store_third(tap, value):
        grads[27 + tap] = value

    grad_taps(turned, cot3, store_third)
    for y in range(4):
        own = spg[y + 1, :, 128:384].astype(jnp.float32)
        rows = slice(y * 128, y * 128 + 128)
        spg3[rows, 0:256] = row_after(own).astype(jnp.bfloat16)
        spg3[rows, 256:512] = own.astype(jnp.bfloat16)
        spg3[rows, 512:768] = row_before(own).astype(jnp.bfloat16)
    turned[...] = cells[1:7, :, 128:640].reshape(768, 512).T

    def store_second(tap, value):
        grads[tap] = value.T

    grad_taps(turned, spg3, store_second)
    lay_filters(filters, lambda a, b, c: k3[9 * a + 3 * b + c], False)
    conv_rows(hidden, slice(0, 512), filters, total, 4)
    for y in range(4):
        done = joined(total, y).astype(jnp.bfloat16)
        for z in range(2):
            output[z, y] = done[:, z * 128 : z * 128 + 128].T


def mid_section(pc, pzl, pzh, pyl, pyh, hidden_grad, cot3, k2, k3, flags):
    return call(
        mid_body,
        [
            ((2, 4, 128, 128), jnp.bfloat16),
            ((54, 128, 128), jnp.bfloat16),
            ((6, 128, 512), jnp.bfloat16),
        ],
        [
            ((8, 128, 768), jnp.bfloat16),
            ((6, 128, 512), jnp.bfloat16),
            ((3, 512, 768), jnp.bfloat16),
            ((768, 768), jnp.float32),
            ((512, 768), jnp.bfloat16),
            ((512, 768), jnp.bfloat16),
        ],
        [pc, pzl, pzh, pyl, pyh, hidden_grad, cot3, k2, k3, flags],
        smem=1,
        flops=7_000_000_000,
        name="mid",
    )


def last_body(spg, k2, xt, bits, first, filters, total, back, full):
    lay_filters(filters, lambda a, b, c: k2[(2 - a) * 9 + (2 - b) * 3 + 2 - c], False)
    conv_rows(spg, slice(0, 512), filters, total, 4)
    for y in range(4):
        grad = joined(total, y).astype(jnp.bfloat16).astype(jnp.float32)
        for z in range(2):
            share = grad[:, z * 128 : z * 128 + 128] * 0.125
            up, down = share.astype(jnp.bfloat16), (share * leak_slope).astype(jnp.bfloat16)
            up, down = up.astype(jnp.float32), down.astype(jnp.float32)
            mask = bits[z, y]
            for zz in range(2):
                for yy in range(2):
                    for par in range(2):
                        bit = mask & (1 << (zz * 4 + yy * 2 + par))
                        row = (2 * y + yy) * 128
                        back[2 * z + zz, row : row + 128, par * 128 : par * 128 + 128] = (
                            jnp.where(bit != 0, up, down).astype(jnp.bfloat16)
                        )
    for b in range(3):
        parts = None
        for z in range(4):
            left = xt[z : z + 3, :, b * 128 : b * 128 + 1024].reshape(768, 1024)
            part = dot(left, back[z])
            parts = part if parts is None else parts + part
        full[...] = parts
        for a in range(3):
            for c in range(3):
                even, odd = ((2, 0), (0, 1), (1, 3))[c]
                low = full[a * 256 + even * 64 : a * 256 + even * 64 + 64, 0:128]
                high = full[a * 256 + odd * 64 : a * 256 + odd * 64 + 64, 128:256]
                tap = (9 * a + 3 * b + c) * 64
                first[tap : tap + 64, :] = (low + high).astype(jnp.bfloat16)
    first[1728:2048, :] = jnp.zeros((320, 128), jnp.bfloat16)


def last_section(spg, k2, xt, bits):
    return call(
        last_body,
        [((2048, 128), jnp.bfloat16)],
        [
            ((3, 512, 768), jnp.bfloat16),
            ((768, 768), jnp.float32),
            ((4, 1024, 256), jnp.bfloat16),
            ((768, 256), jnp.float32),
        ],
        [spg, k2, xt, bits],
        flops=6_000_000_000,
        name="last",
    )[0]


def cot_to_cells(values):
    wide = jnp.pad(values, ((0, 0), (2, 2), (0, 0), (0, 0)))
    parts = jnp.stack([wide[:, 4 * k : 4 * k + 8] for k in range(8)])
    parts = lax.all_to_all(parts.reshape(16, 2, 8, 8, 128), "sx", 0, 0, tiled=True)
    cells = parts.transpose(1, 2, 0, 3, 4).reshape(2, 8, 128, 128)
    return lax.ppermute(cells, both, swap_places(-1))


def output_to_channels(values):
    moved = lax.ppermute(values, both, swap_places(1))
    parts = jnp.swapaxes(moved.reshape(8, 16, 8, 128), 0, 1)
    parts = lax.all_to_all(parts, "sx", 0, 0, tiled=True)
    parts = parts.reshape(8, 2, 2, 4, 8, 128).transpose(1, 2, 0, 3, 4, 5)
    return parts.reshape(4, 32, 8, 128)


def on_device(volume, first_kernel, second_kernel, third_kernel, cotangent):
    sx, sy = lax.axis_index("sx"), lax.axis_index("sy")
    flags = jnp.stack([sx > 0, sx < 15, sy > 0, sy < 7]).astype(jnp.float32)
    vc = jnp.swapaxes(volume, 2, 3)
    vzl, vzh = neighbours(vc[:1], vc[-1:], "sx")
    deep = lambda y: jnp.concatenate([vzl[:, y : y + 1], vc[:, y : y + 1], vzh[:, y : y + 1]])
    vyl, vyh = neighbours(deep(0), deep(7), "sy")
    shares = jnp.concatenate(
        [jnp.swapaxes(second_kernel, 3, 4).reshape(216, 128), third_kernel.reshape(216, 128)]
    )
    filters = lax.all_gather(shares, "sx", axis=0, tiled=True).reshape(16, 54, 8, 128)
    filters = filters.swapaxes(0, 1).reshape(54, 128, 128)
    k2, k3 = filters[:27], filters[27:]
    cc = cot_to_cells(jnp.swapaxes(cotangent, 2, 3))
    cl, ch = neighbours(cc, cc, "sx")
    pooled, bits, xt = first_section(vc, vzl, vzh, vyl, vyh, pair_filters(first_kernel))
    hidden_grad, cot3 = cot_section(cc, cl, ch, k3)
    pzl, pzh = neighbours(pooled, pooled, "sx")
    tall = jnp.concatenate([pzl, pooled, pzh])
    pyl, pyh = neighbours(tall[:, :2], tall[:, 2:], "sy")
    output, grads, spg = mid_section(
        pooled, pzl, pzh, pyl, pyh, hidden_grad, cot3, k2, k3, flags
    )
    first_part = last_section(spg, k2, xt, bits)
    output = jnp.swapaxes(output_to_channels(output), 2, 3)
    share = sum_parts(grads.reshape(54, 16, 8, 128).swapaxes(0, 1).reshape(16, 432, 128), "sx")
    share = sum_parts(jnp.pad(share, ((0, 80), (0, 0))).reshape(8, 64, 128), "sy")
    share = spread_part(share, "sy", 8)[:432].astype(jnp.float32).reshape(2, 3, 3, 3, 8, 128)
    second_grad, third_grad = jnp.swapaxes(share[0], 3, 4), share[1]
    first_sum = spread_part(sum_parts(first_part.reshape(128, 16, 128), both), both, 128)
    first_grad = first_sum[:1728].astype(jnp.float32).reshape(3, 3, 3, 64, 128)
    return (output, first_grad, second_grad, third_grad)


def solution(mesh):
    in_specs = (
        P("sx", "sy", None, None),
        P(),
        P(None, None, None, None, "sx"),
        P(None, None, None, "sx", None),
        P("sy", None, None, "sx"),
    )
    out_specs = (
        P("sy", None, None, "sx"),
        P(),
        P(None, None, None, None, "sx"),
        P(None, None, None, "sx", None),
    )
    return jax.shard_map(
        on_device, mesh=mesh, in_specs=in_specs, out_specs=out_specs, check_vma=False
    )
```

```python
import jax
import jax.numpy as jnp
import numpy as np
from jax import lax
from jax.experimental import pallas as pl
from jax.experimental.pallas import tpu as pltpu
from jax.sharding import PartitionSpec as P

leak_slope = 0.2
vmem_bytes = 56 * 1024 * 1024


def partner_neighbours(first, last):
    low = lax.axis_index("sx") % 2 == 0
    near = lax.ppermute(jnp.where(low, last, first), "sx", [(i, i ^ 1) for i in range(16)])
    far = lax.ppermute(
        jnp.where(low, first, last), "sx", [(i, i - 1 + 2 * (i % 2)) for i in range(1, 15)]
    )
    return jnp.where(low, far, near), jnp.where(low, near, far)


def neighbours(first, last, axis):
    ends = lax.axis_size(axis) - 1
    return (
        lax.ppermute(last, axis, [(i, i + 1) for i in range(ends)]),
        lax.ppermute(first, axis, [(i + 1, i) for i in range(ends)]),
    )


def other_core(values):
    return lax.ppermute(values, "sx", [(i, i ^ 1) for i in range(16)])


def to_chips(parts):
    groups = [list(range(0, 16, 2)), list(range(1, 16, 2))]
    return lax.all_to_all(parts, "sx", 0, 0, axis_index_groups=groups, tiled=True)


def to_sy(parts):
    return lax.all_to_all(parts, "sy", 0, 0, tiled=True)


def repeated(part):
    return jnp.broadcast_to(part[None], (8,) + part.shape)


def sum_first(parts):
    return parts.astype(jnp.float32).sum(0)


def dot(left, right):
    return jnp.dot(left, right, preferred_element_type=jnp.float32)


def row_before(values):
    rows = lax.broadcasted_iota(jnp.int32, values.shape, 0)
    return jnp.where(rows == 0, 0.0, pltpu.roll(values, 1, 0))


def row_after(values):
    count = values.shape[0]
    rows = lax.broadcasted_iota(jnp.int32, values.shape, 0)
    return jnp.where(rows == count - 1, 0.0, pltpu.roll(values, count - 1, 0))


def call(body, outs, scratch, operands, smem=0, flops=0, name=None):
    size = sum(int(np.prod(a.shape)) * a.dtype.itemsize for a in operands)
    size += sum(int(np.prod(shape)) * jnp.dtype(kind).itemsize for shape, kind in outs)
    whole = pl.BlockSpec(memory_space=pltpu.VMEM)
    specs = [whole] * (len(operands) - smem) + [pl.BlockSpec(memory_space=pltpu.SMEM)] * smem
    return pl.pallas_call(
        body,
        out_shape=[jax.ShapeDtypeStruct(shape, kind) for shape, kind in outs],
        in_specs=specs,
        out_specs=[whole] * len(outs),
        scratch_shapes=[pltpu.VMEM(shape, kind) for shape, kind in scratch],
        compiler_params=pltpu.CompilerParams(vmem_limit_bytes=vmem_bytes),
        cost_estimate=pl.CostEstimate(flops=flops, bytes_accessed=size, transcendentals=0),
        name=name,
    )(*operands)


def pair_select():
    sel = np.zeros((256, 4, 128), np.float32)
    for k, offset in enumerate((0, 1, -1, 2)):
        for p in range(128):
            if 0 <= 2 * p + offset < 256:
                sel[2 * p + offset, k, p] = 1
    return jnp.asarray(sel.reshape(256, 512), jnp.bfloat16)


def pair_filters(kernel):
    taps = kernel.reshape(9, 3, 64, 128)
    none = jnp.zeros((9, 64, 128), kernel.dtype)
    even = jnp.concatenate([taps[:, 1], taps[:, 2], taps[:, 0], none], axis=1)
    odd = jnp.concatenate([taps[:, 0], taps[:, 1], none, taps[:, 2]], axis=1)
    return jnp.concatenate([even, odd], axis=2)


def first_body(vc, vzl, vzh, vyl, vyh, w1, sel, pooled, bits, xt, xc, acc):
    for z in range(6):
        rows = vzl[0] if z == 0 else vzh[0] if z == 5 else vc[z - 1]
        got = dot(rows.reshape(512, 256), sel[...]).astype(jnp.bfloat16)
        low = dot(vyl[z, 0], sel[...]).astype(jnp.bfloat16)
        high = dot(vyh[z, 0], sel[...]).astype(jnp.bfloat16)
        for k in range(4):
            lanes = slice(k * 128, k * 128 + 128)
            place = slice(k * 64, k * 64 + 64)
            xt[z, place, 0:128] = low[:, lanes]
            xt[z, place, 1152:1280] = high[:, lanes]
            for y in range(8):
                xt[z, place, (y + 1) * 128 : (y + 2) * 128] = got[y * 64 : y * 64 + 64, lanes]
        xc[z] = xt[z].T

    @pl.loop(0, 2)
    def _(zp):
        for zz in range(2):
            total = None
            for a in range(3):
                for b in range(3):
                    part = dot(xc[2 * zp + zz + a, b * 128 : b * 128 + 1024, :], w1[3 * a + b])
                    total = part if total is None else total + part
            acc[zz] = total
        for yp in range(4):
            mean = jnp.zeros((128, 128), jnp.float32)
            mask = jnp.zeros((128, 128), jnp.int32)
            for zz in range(2):
                for yy in range(2):
                    for par in range(2):
                        row = (2 * yp + yy) * 128
                        v = acc[zz, row : row + 128, par * 128 : par * 128 + 128]
                        up = v > 0
                        mean += jnp.where(up, v, leak_slope * v)
                        mask |= jnp.where(up, 1 << (zz * 4 + yy * 2 + par), 0)
            pooled[zp, yp] = (mean * 0.125).astype(jnp.bfloat16)
            bits[zp, yp] = mask


def first_section(vc, vzl, vzh, vyl, vyh, w1):
    return call(
        first_body,
        [
            ((2, 4, 128, 128), jnp.bfloat16),
            ((2, 4, 128, 128), jnp.int32),
            ((6, 256, 1280), jnp.bfloat16),
        ],
        [((6, 1280, 256), jnp.bfloat16), ((2, 1024, 256), jnp.float32)],
        [vc, vzl, vzh, vyl, vyh, w1, pair_select()],
        flops=5_000_000_000,
        name="first",
    )


def lay_filters(place, tap_of, turn):
    for b in range(3):
        for four in range(4):
            for c in range(3):
                for two in range(2):
                    a = four - two
                    lanes = slice(c * 256 + two * 128, c * 256 + two * 128 + 128)
                    block = (b, slice(four * 128, four * 128 + 128), lanes)
                    if 0 <= a < 3:
                        tap = tap_of(a, b, c)
                        place[block] = tap.T if turn else tap
                    else:
                        place[block] = jnp.zeros((128, 128), jnp.bfloat16)


def conv_rows(source, lanes, filters, total, count):
    rows = count * 128
    parts = None
    for b in range(3):
        part = dot(source[b : b + count, :, lanes].reshape(rows, 512), filters[b])
        parts = part if parts is None else parts + part
    total[0:rows, :] = parts


def joined(total, y):
    rows = slice(y * 128, y * 128 + 128)
    return (
        row_before(total[rows, 0:256]) + total[rows, 256:512] + row_after(total[rows, 512:768])
    )


def cot_body(cc, cl, ch, k3, hidden_grad, cot3, cells, filters, total):
    for z in range(6):
        part = (cl, cc, ch)[z // 2]
        for y in range(8):
            cells[y, :, z * 128 : z * 128 + 128] = part[z % 2, y].T
    lay_filters(filters, lambda a, b, c: k3[(2 - a) * 9 + (2 - b) * 3 + 2 - c], True)
    for j in range(2):
        conv_rows(cells, slice(j * 256, j * 256 + 512), filters, total, 6)
        for y in range(6):
            hidden_grad[y, :, j * 256 : j * 256 + 256] = joined(total, y)
    for y in range(4):
        own = cells[y + 2, :, 256:512].astype(jnp.float32)
        rows = slice(y * 128, y * 128 + 128)
        cot3[rows, 0:256] = row_after(own).astype(jnp.bfloat16)
        cot3[rows, 256:512] = own.astype(jnp.bfloat16)
        cot3[rows, 512:768] = row_before(own).astype(jnp.bfloat16)


def cot_section(cc, cl, ch, k3):
    return call(
        cot_body,
        [((6, 128, 512), jnp.float32), ((512, 768), jnp.bfloat16)],
        [
            ((8, 128, 768), jnp.bfloat16),
            ((3, 512, 768), jnp.bfloat16),
            ((768, 768), jnp.float32),
        ],
        [cc, cl, ch, k3],
        flops=3_600_000_000,
        name="cot",
    )


def grad_taps(turned, cot3, store):
    for b in range(3):
        full = dot(turned[:, b * 128 : b * 128 + 512], cot3[...])
        for a in range(3):
            for c in range(3):
                low = full[a * 128 : a * 128 + 128, c * 256 : c * 256 + 128]
                high = full[a * 128 + 128 : a * 128 + 256, c * 256 + 128 : c * 256 + 256]
                store(9 * a + 3 * b + c, low + high)


def mid_body(
    pc, pzl, pzh, pyl, pyh, hidden_grad, cot3, k2, k3, flags,
    maps, spg, cells, hidden, filters, total, spg3, turned,
):
    for z in range(6):
        lanes = slice(z * 128, z * 128 + 128)
        part = (pzl, pc, pzh)[z // 2]
        for y in range(2):
            cells[y, :, lanes] = pyl[z, y]
            cells[y + 6, :, lanes] = pyh[z, y]
        for y in range(4):
            cells[y + 2, :, lanes] = part[z % 2, y]
    lay_filters(filters, lambda a, b, c: k2[9 * a + 3 * b + c], True)
    lane = lax.broadcasted_iota(jnp.int32, (128, 256), 1)
    for j in range(2):
        conv_rows(cells, slice(j * 256, j * 256 + 512), filters, total, 6)
        edge = lane < 128 if j == 0 else lane >= 128
        inside = jnp.where(edge, flags[j], 1.0)
        for y in range(6):
            pre = joined(total, y)
            keep = inside * flags[2] if y == 0 else inside * flags[3] if y == 5 else inside
            lanes = slice(j * 256, j * 256 + 256)
            up = pre > 0
            hidden[y, :, lanes] = (jnp.where(up, pre, leak_slope * pre) * keep).astype(
                jnp.bfloat16
            )
            back = hidden_grad[y, :, lanes]
            spg[y, :, lanes] = (jnp.where(up, back, leak_slope * back) * keep).astype(
                jnp.bfloat16
            )
    turned[...] = hidden[...].reshape(768, 512).T

    def store(place, value):
        for i in range(16):
            maps[i % 2, i // 2, place] = value[i * 8 : i * 8 + 8]

    def store_third(tap, value):
        store(27 + tap, value)

    grad_taps(turned, cot3, store_third)
    for y in range(4):
        own = spg[y + 1, :, 128:384].astype(jnp.float32)
        rows = slice(y * 128, y * 128 + 128)
        spg3[rows, 0:256] = row_after(own).astype(jnp.bfloat16)
        spg3[rows, 256:512] = own.astype(jnp.bfloat16)
        spg3[rows, 512:768] = row_before(own).astype(jnp.bfloat16)
    turned[...] = cells[1:7, :, 128:640].reshape(768, 512).T

    def store_second(tap, value):
        store(tap, value.T)

    grad_taps(turned, spg3, store_second)
    lay_filters(filters, lambda a, b, c: k3[9 * a + 3 * b + c], False)
    conv_rows(hidden, slice(0, 512), filters, total, 4)
    for y in range(4):
        done = joined(total, y)
        for z in range(2):
            store(54 + z * 4 + y, done[:, z * 128 : z * 128 + 128].T)


def mid_section(pc, pzl, pzh, pyl, pyh, hidden_grad, cot3, k2, k3, flags):
    return call(
        mid_body,
        [
            ((2, 8, 62, 8, 128), jnp.float32),
            ((6, 128, 512), jnp.bfloat16),
        ],
        [
            ((8, 128, 768), jnp.bfloat16),
            ((6, 128, 512), jnp.bfloat16),
            ((3, 512, 768), jnp.bfloat16),
            ((768, 768), jnp.float32),
            ((512, 768), jnp.bfloat16),
            ((512, 768), jnp.bfloat16),
        ],
        [pc, pzl, pzh, pyl, pyh, hidden_grad, cot3, k2, k3, flags],
        smem=1,
        flops=7_000_000_000,
        name="mid",
    )


def last_body(spg, k2, xt, bits, first, filters, total, back, full):
    lay_filters(filters, lambda a, b, c: k2[(2 - a) * 9 + (2 - b) * 3 + 2 - c], False)
    conv_rows(spg, slice(0, 512), filters, total, 4)
    for y in range(4):
        grad = joined(total, y).astype(jnp.bfloat16).astype(jnp.float32)
        for z in range(2):
            share = grad[:, z * 128 : z * 128 + 128] * 0.125
            up, down = share.astype(jnp.bfloat16), (share * leak_slope).astype(jnp.bfloat16)
            up, down = up.astype(jnp.float32), down.astype(jnp.float32)
            mask = bits[z, y]
            for zz in range(2):
                for yy in range(2):
                    for par in range(2):
                        bit = mask & (1 << (zz * 4 + yy * 2 + par))
                        row = (2 * y + yy) * 128
                        back[2 * z + zz, row : row + 128, par * 128 : par * 128 + 128] = (
                            jnp.where(bit != 0, up, down).astype(jnp.bfloat16)
                        )
    for b in range(3):
        parts = None
        for z in range(4):
            left = xt[z : z + 3, :, b * 128 : b * 128 + 1024].reshape(768, 1024)
            part = dot(left, back[z])
            parts = part if parts is None else parts + part
        full[...] = parts
        for a in range(3):
            for c in range(3):
                even, odd = ((2, 0), (0, 1), (1, 3))[c]
                low = full[a * 256 + even * 64 : a * 256 + even * 64 + 64, 0:128]
                high = full[a * 256 + odd * 64 : a * 256 + odd * 64 + 64, 128:256]
                tap = 9 * a + 3 * b + c
                first[tap // 16, tap % 16 * 64 : tap % 16 * 64 + 64, :] = low + high
    first[1, 704:1024, :] = jnp.zeros((320, 128), jnp.float32)


def last_section(spg, k2, xt, bits):
    return call(
        last_body,
        [((2, 1024, 128), jnp.float32)],
        [
            ((3, 512, 768), jnp.bfloat16),
            ((768, 768), jnp.float32),
            ((4, 1024, 256), jnp.bfloat16),
            ((768, 256), jnp.float32),
        ],
        [spg, k2, xt, bits],
        flops=6_000_000_000,
        name="last",
    )[0]


def cot_rows(values):
    own = values.reshape(4, 8, 4, 8, 128)
    below = jnp.pad(own[:, :7, 2:], ((0, 0), (1, 0), (0, 0), (0, 0), (0, 0)))
    above = jnp.pad(own[:, 1:, :2], ((0, 0), (0, 1), (0, 0), (0, 0), (0, 0)))
    return jnp.swapaxes(jnp.concatenate([below, own, above], axis=2), 0, 1)


def after(values, *done):
    return lax.optimization_barrier((values,) + done)[0]


def on_device(volume, first_kernel, second_kernel, third_kernel, cotangent):
    sx, sy = lax.axis_index("sx"), lax.axis_index("sy")
    core = sx % 2
    flags = jnp.stack([sx > 0, sx < 15, sy > 0, sy < 7]).astype(jnp.float32)
    vc = jnp.swapaxes(volume, 2, 3)
    vzl, vzh = partner_neighbours(vc[:1], vc[-1:])
    deep = lambda y: jnp.concatenate([vzl[:, y : y + 1], vc[:, y : y + 1], vzh[:, y : y + 1]])
    vyl, vyh = neighbours(deep(0), deep(7), "sy")
    shares = jnp.concatenate(
        [jnp.swapaxes(second_kernel, 3, 4).reshape(216, 128), third_kernel.reshape(216, 128)]
    )
    filters = lax.all_gather(shares, "sx", axis=0, tiled=True).reshape(16, 54, 8, 128)
    filters = filters.swapaxes(0, 1).reshape(54, 128, 128)
    k2, k3 = filters[:27], filters[27:]
    cot_tall = to_sy(after(cot_rows(jnp.swapaxes(cotangent, 2, 3)), vzl, vzh))
    cot_parts = lax.all_to_all(cot_tall.reshape(16, 2, 8, 8, 128), "sx", 0, 0, tiled=True)
    cc = cot_parts.transpose(1, 2, 0, 3, 4).reshape(2, 8, 128, 128)
    cl, ch = partner_neighbours(cc, cc)
    w1 = after(pair_filters(first_kernel), cot_tall)
    pooled, bits, xt = first_section(vc, vzl, vzh, vyl, vyh, w1)
    hidden_grad, cot3 = cot_section(cc, cl, ch, k3)
    pzl, pzh = partner_neighbours(pooled, pooled)
    tall = jnp.concatenate([pzl, pooled, pzh])
    pyl, pyh = neighbours(tall[:, :2], tall[:, 2:], "sy")
    maps, spg = mid_section(pooled, pzl, pzh, pyl, pyh, hidden_grad, cot3, k2, k3, flags)
    from_other = other_core(maps[1 - core].astype(jnp.bfloat16))
    own = maps[core]
    first_part = last_section(spg, k2, xt, bits)
    first_from = other_core(first_part[1 - core].astype(jnp.bfloat16))
    first_half = first_part[core] + first_from.astype(jnp.float32)
    grads = own[:, :54] + from_other[:, :54].astype(jnp.float32)
    mine, theirs = own[:, 54:].astype(jnp.bfloat16), from_other[:, 54:]
    parts = jnp.concatenate(
        [
            grads.astype(jnp.bfloat16),
            jnp.where(core == 0, mine, theirs),
            jnp.where(core == 0, theirs, mine),
            first_half.astype(jnp.bfloat16).reshape(8, 16, 8, 128),
        ],
        axis=1,
    )
    parts = to_chips(parts)
    grads = jnp.pad(sum_first(parts[:, :54]), ((0, 2), (0, 0), (0, 0)))
    first_half = sum_first(parts[:, 70:])
    parts = jnp.concatenate(
        [
            grads.astype(jnp.bfloat16).reshape(8, 7, 8, 128),
            first_half.astype(jnp.bfloat16).reshape(8, 2, 8, 128),
            parts[:, 54:70],
        ],
        axis=1,
    )
    parts = to_sy(parts)
    output = parts[:, 9:].reshape(8, 4, 4, 8, 128).swapaxes(0, 1).reshape(4, 32, 8, 128)
    share = to_sy(repeated(sum_first(parts[:, :9]).astype(jnp.bfloat16)))
    grads = share[:, :7].reshape(56, 8, 128)[:54].astype(jnp.float32)
    grads = grads.reshape(2, 3, 3, 3, 8, 128)
    half = to_chips(repeated(share[:, 7:].reshape(128, 128))).reshape(1024, 128)
    other = other_core(half)
    first_grad = jnp.concatenate(
        [jnp.where(core == 0, half, other), jnp.where(core == 0, other, half)[:704]]
    )
    first_grad = first_grad.astype(jnp.float32).reshape(3, 3, 3, 64, 128)
    return (jnp.swapaxes(output, 2, 3), first_grad, jnp.swapaxes(grads[0], 3, 4), grads[1])


def solution(mesh):
    in_specs = (
        P("sx", "sy", None, None),
        P(),
        P(None, None, None, None, "sx"),
        P(None, None, None, "sx", None),
        P("sy", None, None, "sx"),
    )
    out_specs = (
        P("sy", None, None, "sx"),
        P(),
        P(None, None, None, None, "sx"),
        P(None, None, None, "sx", None),
    )
    return jax.shard_map(
        on_device, mesh=mesh, in_specs=in_specs, out_specs=out_specs, check_vma=False
    )
```

```python
import jax
import jax.numpy as jnp
import numpy as np
from jax import lax
from jax.experimental import pallas as pl
from jax.experimental.pallas import tpu as pltpu
from jax.sharding import PartitionSpec as P

leak_slope = 0.2
same_core = [list(range(0, 16, 2)), list(range(1, 16, 2))]
mib = 1024 * 1024


def partner_neighbours(first, last):
    low = lax.axis_index("sx") % 2 == 0
    near = lax.ppermute(jnp.where(low, last, first), "sx", [(i, i ^ 1) for i in range(16)])
    far = lax.ppermute(
        jnp.where(low, first, last), "sx", [(i, i - 1 + 2 * (i % 2)) for i in range(1, 15)]
    )
    return jnp.where(low, far, near), jnp.where(low, near, far), near


def neighbours(first, last, axis):
    ends = lax.axis_size(axis) - 1
    return (
        lax.ppermute(last, axis, [(i, i + 1) for i in range(ends)]),
        lax.ppermute(first, axis, [(i + 1, i) for i in range(ends)]),
    )


def other_core(values):
    return lax.ppermute(values, "sx", [(i, i ^ 1) for i in range(16)])


def to_chips(parts):
    return lax.all_to_all(parts, "sx", 0, 0, axis_index_groups=same_core, tiled=True)


def to_sy(parts):
    return lax.all_to_all(parts, "sy", 0, 0, tiled=True)


def repeated(part, count):
    return jnp.broadcast_to(part[None], (count,) + part.shape)


def sum_first(parts):
    return parts.astype(jnp.float32).sum(0)


def dot(left, right):
    return jnp.dot(left, right, preferred_element_type=jnp.float32)


def row_before(values):
    rows = lax.broadcasted_iota(jnp.int32, values.shape, 0)
    return jnp.where(rows == 0, 0.0, pltpu.roll(values, 1, 0))


def row_after(values):
    count = values.shape[0]
    rows = lax.broadcasted_iota(jnp.int32, values.shape, 0)
    return jnp.where(rows == count - 1, 0.0, pltpu.roll(values, count - 1, 0))


def call(body, outs, scratch, operands, smem=0, flops=0, vmem=24, name=None):
    size = sum(int(np.prod(a.shape)) * a.dtype.itemsize for a in operands)
    size += sum(int(np.prod(shape)) * jnp.dtype(kind).itemsize for shape, kind in outs)
    whole = pl.BlockSpec(memory_space=pltpu.VMEM)
    specs = [whole] * (len(operands) - smem) + [pl.BlockSpec(memory_space=pltpu.SMEM)] * smem
    return pl.pallas_call(
        body,
        out_shape=[jax.ShapeDtypeStruct(shape, kind) for shape, kind in outs],
        in_specs=specs,
        out_specs=[whole] * len(outs),
        scratch_shapes=[pltpu.VMEM(shape, kind) for shape, kind in scratch],
        compiler_params=pltpu.CompilerParams(vmem_limit_bytes=vmem * mib),
        cost_estimate=pl.CostEstimate(flops=flops, bytes_accessed=size, transcendentals=0),
        name=name,
    )(*operands)


def pair_select():
    sel = np.zeros((256, 4, 128), np.float32)
    for k, offset in enumerate((0, 1, -1, 2)):
        for p in range(128):
            if 0 <= 2 * p + offset < 256:
                sel[2 * p + offset, k, p] = 1
    return jnp.asarray(sel.reshape(256, 512), jnp.bfloat16)


def pair_filters(kernel):
    taps = kernel.reshape(9, 3, 64, 128)
    none = jnp.zeros((9, 64, 128), kernel.dtype)
    even = jnp.concatenate([taps[:, 1], taps[:, 2], taps[:, 0], none], axis=1)
    odd = jnp.concatenate([taps[:, 0], taps[:, 1], none, taps[:, 2]], axis=1)
    return jnp.concatenate([even, odd], axis=2)


def first_body(vc, vzl, vzh, vyl, vyh, w1, sel, pooled, bits, xt, xc, acc):
    for z in range(6):
        rows = vzl[0] if z == 0 else vzh[0] if z == 5 else vc[z - 1]
        got = dot(rows.reshape(512, 256), sel[...]).astype(jnp.bfloat16)
        low = dot(vyl[z, 0], sel[...]).astype(jnp.bfloat16)
        high = dot(vyh[z, 0], sel[...]).astype(jnp.bfloat16)
        for k in range(4):
            lanes = slice(k * 128, k * 128 + 128)
            place = slice(k * 64, k * 64 + 64)
            xt[z, place, 0:128] = low[:, lanes]
            xt[z, place, 1152:1280] = high[:, lanes]
            for y in range(8):
                xt[z, place, (y + 1) * 128 : (y + 2) * 128] = got[y * 64 : y * 64 + 64, lanes]
        xc[z] = xt[z].T

    @pl.loop(0, 2)
    def _(zp):
        for zz in range(2):
            total = None
            for a in range(3):
                for b in range(3):
                    part = dot(xc[2 * zp + zz + a, b * 128 : b * 128 + 1024, :], w1[3 * a + b])
                    total = part if total is None else total + part
            acc[zz] = total
        for yp in range(4):
            mean = jnp.zeros((128, 128), jnp.float32)
            mask = jnp.zeros((128, 128), jnp.int32)
            for zz in range(2):
                for yy in range(2):
                    for par in range(2):
                        row = (2 * yp + yy) * 128
                        v = acc[zz, row : row + 128, par * 128 : par * 128 + 128]
                        up = v > 0
                        mean += jnp.where(up, v, leak_slope * v)
                        mask |= jnp.where(up, 1 << (zz * 4 + yy * 2 + par), 0)
            pooled[zp, yp] = (mean * 0.125).astype(jnp.bfloat16)
            bits[zp, yp] = mask


def first_section(vc, vzl, vzh, vyl, vyh, w1):
    return call(
        first_body,
        [
            ((2, 4, 128, 128), jnp.bfloat16),
            ((2, 4, 128, 128), jnp.int32),
            ((6, 256, 1280), jnp.bfloat16),
        ],
        [((6, 1280, 256), jnp.bfloat16), ((2, 1024, 256), jnp.float32)],
        [vc, vzl, vzh, vyl, vyh, w1, pair_select()],
        flops=5_000_000_000,
        name="first",
    )


def lay_filters(place, tap_of, turn):
    for b in range(3):
        for four in range(4):
            for c in range(3):
                for two in range(2):
                    a = four - two
                    lanes = slice(c * 256 + two * 128, c * 256 + two * 128 + 128)
                    block = (b, slice(four * 128, four * 128 + 128), lanes)
                    if 0 <= a < 3:
                        tap = tap_of(a, b, c)
                        place[block] = tap.T if turn else tap
                    else:
                        place[block] = jnp.zeros((128, 128), jnp.bfloat16)


def conv_rows(source, lanes, filters, total, count):
    rows = count * 128
    parts = None
    for b in range(3):
        part = dot(source[b : b + count, :, lanes].reshape(rows, 512), filters[b])
        parts = part if parts is None else parts + part
    total[0:rows, :] = parts


def joined(total, y):
    rows = slice(y * 128, y * 128 + 128)
    return (
        row_before(total[rows, 0:256]) + total[rows, 256:512] + row_after(total[rows, 512:768])
    )


def cot_body(half, near, k3, core, hidden_grad, cot3, cells, filters, total):
    first = core[0] * 2
    for z in range(4):
        for y in range(8):
            lanes = pl.ds(pl.multiple_of((first + z) * 128, 128), 128)
            cells[y, :, lanes] = half[z, y].T
    for z in range(2):
        for y in range(8):
            lanes = pl.ds(pl.multiple_of((4 - 2 * first + z) * 128, 128), 128)
            cells[y, :, lanes] = near[z, y].T
    lay_filters(filters, lambda a, b, c: k3[(2 - a) * 9 + (2 - b) * 3 + 2 - c], True)
    for j in range(2):
        conv_rows(cells, slice(j * 256, j * 256 + 512), filters, total, 6)
        for y in range(6):
            hidden_grad[y, :, j * 256 : j * 256 + 256] = joined(total, y)
    for y in range(4):
        own = cells[y + 2, :, 256:512].astype(jnp.float32)
        rows = slice(y * 128, y * 128 + 128)
        cot3[rows, 0:256] = row_after(own).astype(jnp.bfloat16)
        cot3[rows, 256:512] = own.astype(jnp.bfloat16)
        cot3[rows, 512:768] = row_before(own).astype(jnp.bfloat16)


def cot_section(half, near, core, k3):
    return call(
        cot_body,
        [((6, 128, 512), jnp.float32), ((512, 768), jnp.bfloat16)],
        [
            ((8, 128, 768), jnp.bfloat16),
            ((3, 512, 768), jnp.bfloat16),
            ((768, 768), jnp.float32),
        ],
        [half, near, k3, core.reshape(1)],
        smem=1,
        flops=3_600_000_000,
        name="cot",
    )


def grad_taps(turned, cot3, store):
    for b in range(3):
        full = dot(turned[:, b * 128 : b * 128 + 512], cot3[...])
        for a in range(3):
            for c in range(3):
                low = full[a * 128 : a * 128 + 128, c * 256 : c * 256 + 128]
                high = full[a * 128 + 128 : a * 128 + 256, c * 256 + 128 : c * 256 + 256]
                store(9 * a + 3 * b + c, low + high)


def mid_body(
    pc, pzl, pzh, pyl, pyh, hidden_grad, cot3, k2, k3, flags,
    maps, spg, cells, hidden, filters, total, spg3, turned,
):
    for z in range(6):
        lanes = slice(z * 128, z * 128 + 128)
        part = (pzl, pc, pzh)[z // 2]
        for y in range(2):
            cells[y, :, lanes] = pyl[z, y]
            cells[y + 6, :, lanes] = pyh[z, y]
        for y in range(4):
            cells[y + 2, :, lanes] = part[z % 2, y]
    lay_filters(filters, lambda a, b, c: k2[9 * a + 3 * b + c], True)
    lane = lax.broadcasted_iota(jnp.int32, (128, 256), 1)
    for j in range(2):
        conv_rows(cells, slice(j * 256, j * 256 + 512), filters, total, 6)
        edge = lane < 128 if j == 0 else lane >= 128
        inside = jnp.where(edge, flags[j], 1.0)
        for y in range(6):
            pre = joined(total, y)
            keep = inside * flags[2] if y == 0 else inside * flags[3] if y == 5 else inside
            lanes = slice(j * 256, j * 256 + 256)
            up = pre > 0
            hidden[y, :, lanes] = (jnp.where(up, pre, leak_slope * pre) * keep).astype(
                jnp.bfloat16
            )
            back = hidden_grad[y, :, lanes]
            spg[y, :, lanes] = (jnp.where(up, back, leak_slope * back) * keep).astype(
                jnp.bfloat16
            )
    turned[...] = hidden[...].reshape(768, 512).T

    def store(place, value):
        for i in range(16):
            maps[i % 2, i // 2, place] = value[i * 8 : i * 8 + 8]

    def store_third(tap, value):
        store(27 + tap, value)

    grad_taps(turned, cot3, store_third)
    store(54, jnp.zeros((128, 128), jnp.float32))
    store(55, jnp.zeros((128, 128), jnp.float32))
    for y in range(4):
        own = spg[y + 1, :, 128:384].astype(jnp.float32)
        rows = slice(y * 128, y * 128 + 128)
        spg3[rows, 0:256] = row_after(own).astype(jnp.bfloat16)
        spg3[rows, 256:512] = own.astype(jnp.bfloat16)
        spg3[rows, 512:768] = row_before(own).astype(jnp.bfloat16)
    turned[...] = cells[1:7, :, 128:640].reshape(768, 512).T

    def store_second(tap, value):
        store(tap, value.T)

    grad_taps(turned, spg3, store_second)
    lay_filters(filters, lambda a, b, c: k3[9 * a + 3 * b + c], False)
    conv_rows(hidden, slice(0, 512), filters, total, 4)
    for y in range(4):
        done = joined(total, y)
        for z in range(2):
            store(56 + z * 4 + y, done[:, z * 128 : z * 128 + 128].T)


def mid_section(pc, pzl, pzh, pyl, pyh, hidden_grad, cot3, k2, k3, flags):
    return call(
        mid_body,
        [
            ((2, 8, 64, 8, 128), jnp.float32),
            ((6, 128, 512), jnp.bfloat16),
        ],
        [
            ((8, 128, 768), jnp.bfloat16),
            ((6, 128, 512), jnp.bfloat16),
            ((3, 512, 768), jnp.bfloat16),
            ((768, 768), jnp.float32),
            ((512, 768), jnp.bfloat16),
            ((512, 768), jnp.bfloat16),
        ],
        [pc, pzl, pzh, pyl, pyh, hidden_grad, cot3, k2, k3, flags],
        smem=1,
        flops=7_000_000_000,
        vmem=32,
        name="mid",
    )


def last_body(spg, k2, xt, bits, first, filters, total, back, full):
    lay_filters(filters, lambda a, b, c: k2[(2 - a) * 9 + (2 - b) * 3 + 2 - c], False)
    conv_rows(spg, slice(0, 512), filters, total, 4)
    for y in range(4):
        grad = joined(total, y).astype(jnp.bfloat16).astype(jnp.float32)
        for z in range(2):
            share = grad[:, z * 128 : z * 128 + 128] * 0.125
            up, down = share.astype(jnp.bfloat16), (share * leak_slope).astype(jnp.bfloat16)
            up, down = up.astype(jnp.float32), down.astype(jnp.float32)
            mask = bits[z, y]
            for zz in range(2):
                for yy in range(2):
                    for par in range(2):
                        bit = mask & (1 << (zz * 4 + yy * 2 + par))
                        row = (2 * y + yy) * 128
                        back[2 * z + zz, row : row + 128, par * 128 : par * 128 + 128] = (
                            jnp.where(bit != 0, up, down).astype(jnp.bfloat16)
                        )
    for b in range(3):
        parts = None
        for z in range(4):
            left = xt[z : z + 3, :, b * 128 : b * 128 + 1024].reshape(768, 1024)
            part = dot(left, back[z])
            parts = part if parts is None else parts + part
        full[...] = parts
        for a in range(3):
            for c in range(3):
                even, odd = ((2, 0), (0, 1), (1, 3))[c]
                low = full[a * 256 + even * 64 : a * 256 + even * 64 + 64, 0:128]
                high = full[a * 256 + odd * 64 : a * 256 + odd * 64 + 64, 128:256]
                tap = 9 * a + 3 * b + c
                row = tap // 4 * 128 + tap % 2 * 64
                first[tap // 2 % 2, row : row + 64, :] = low + high
    first[1, 832:1024, :] = jnp.zeros((192, 128), jnp.float32)
    first[0, 960:1024, :] = jnp.zeros((64, 128), jnp.float32)
    first[0, 896:960, :] = jnp.zeros((64, 128), jnp.float32)


def last_section(spg, k2, xt, bits):
    return call(
        last_body,
        [((2, 1024, 128), jnp.float32)],
        [
            ((3, 512, 768), jnp.bfloat16),
            ((768, 768), jnp.float32),
            ((4, 1024, 256), jnp.bfloat16),
            ((768, 256), jnp.float32),
        ],
        [spg, k2, xt, bits],
        flops=6_000_000_000,
        name="last",
    )[0]


def cot_rows(values):
    own = values.reshape(4, 8, 4, 8, 128)
    below = jnp.pad(own[:, :7, 2:], ((0, 0), (1, 0), (0, 0), (0, 0), (0, 0)))
    above = jnp.pad(own[:, 1:, :2], ((0, 0), (0, 1), (0, 0), (0, 0), (0, 0)))
    return jnp.swapaxes(jnp.concatenate([below, own, above], axis=2), 0, 1)


def cot_deep(values):
    wide = jnp.pad(values.reshape(32, 8, 8, 128), ((2, 2), (0, 0), (0, 0), (0, 0)))
    wide = wide.reshape(9, 4, 8, 8, 128)
    return jnp.stack([wide[:8], wide[1:]], axis=1).reshape(16, 4, 8, 8, 128)


def after(values, *done):
    return lax.optimization_barrier((values,) + done)[0]


def on_device(volume, first_kernel, second_kernel, third_kernel, cotangent):
    sx, sy = lax.axis_index("sx"), lax.axis_index("sy")
    core = sx % 2
    flags = jnp.stack([sx > 0, sx < 15, sy > 0, sy < 7]).astype(jnp.float32)
    shares = jnp.concatenate(
        [jnp.swapaxes(second_kernel, 3, 4).reshape(216, 128), third_kernel.reshape(216, 128)]
    )
    filters = lax.all_gather(shares, "sx", axis=0, tiled=True)
    vc = jnp.swapaxes(volume, 2, 3)
    vzl, vzh, near = partner_neighbours(after(vc[:1], shares), vc[-1:])
    deep = lambda y: jnp.concatenate([vzl[:, y : y + 1], vc[:, y : y + 1], vzh[:, y : y + 1]])
    vyl, vyh = neighbours(deep(0), deep(7), "sy")
    cot_tall = to_sy(after(cot_rows(jnp.swapaxes(cotangent, 2, 3)), near))
    cot_parts = lax.all_to_all(cot_deep(cot_tall), "sx", 0, 0, tiled=True)
    cot_half = cot_parts.transpose(1, 2, 0, 3, 4).reshape(4, 8, 128, 128)
    cot_near = other_core(jnp.where(core == 0, cot_half[2:], cot_half[:2]))
    w1 = after(pair_filters(first_kernel), cot_tall)
    pooled, bits, xt = first_section(vc, vzl, vzh, vyl, vyh, w1)
    pzl, pzh, _ = partner_neighbours(pooled, pooled)
    filters = filters.reshape(16, 54, 8, 128).swapaxes(0, 1).reshape(54, 128, 128)
    k2, k3 = filters[:27], filters[27:]
    hidden_grad, cot3 = cot_section(cot_half, cot_near, core, k3)
    tall = jnp.concatenate([pzl, pooled, pzh])
    pyl, pyh = neighbours(tall[:, :2], tall[:, 2:], "sy")
    maps, spg = mid_section(pooled, pzl, pzh, pyl, pyh, hidden_grad, cot3, k2, k3, flags)
    from_other = other_core(maps[1 - core].astype(jnp.bfloat16))
    own = maps[core]
    mine, theirs = own[:, 56:].astype(jnp.bfloat16), from_other[:, 56:]
    first_part = last_section(spg, k2, xt, bits)
    first_from = other_core(first_part[1 - core].astype(jnp.bfloat16))
    first_half = first_part[core] + first_from.astype(jnp.float32)
    grads = own[:, :56] + from_other[:, :56].astype(jnp.float32)
    parts = jnp.concatenate(
        [
            grads.astype(jnp.bfloat16),
            jnp.where(core == 0, mine, theirs),
            jnp.where(core == 0, theirs, mine),
            first_half.astype(jnp.bfloat16).reshape(8, 16, 8, 128),
        ],
        axis=1,
    )
    parts = to_chips(parts)
    parts = jnp.concatenate(
        [
            sum_first(parts[:, :56]).astype(jnp.bfloat16).reshape(8, 7, 8, 128),
            sum_first(parts[:, 72:]).astype(jnp.bfloat16).reshape(8, 2, 8, 128),
            parts[:, 56:72],
        ],
        axis=1,
    )
    parts = to_sy(parts)
    output = parts[:, 9:].reshape(8, 4, 4, 8, 128).swapaxes(0, 1).reshape(4, 32, 8, 128)
    share = to_sy(repeated(sum_first(parts[:, :9]).astype(jnp.bfloat16), 8))
    grads = share[:, :7].reshape(56, 8, 128)[:54].astype(jnp.float32)
    grads = grads.reshape(2, 3, 3, 3, 8, 128)
    first_grad = repeated(share[:, 7:].reshape(128, 128), 16)
    first_grad = lax.all_to_all(first_grad, "sx", 0, 0, tiled=True).reshape(2048, 128)[:1728]
    first_grad = first_grad.astype(jnp.float32).reshape(3, 3, 3, 64, 128)
    return (jnp.swapaxes(output, 2, 3), first_grad, jnp.swapaxes(grads[0], 3, 4), grads[1])


def solution(mesh):
    in_specs = (
        P("sx", "sy", None, None),
        P(),
        P(None, None, None, None, "sx"),
        P(None, None, None, "sx", None),
        P("sy", None, None, "sx"),
    )
    out_specs = (
        P("sy", None, None, "sx"),
        P(),
        P(None, None, None, None, "sx"),
        P(None, None, None, "sx", None),
    )
    return jax.shard_map(
        on_device, mesh=mesh, in_specs=in_specs, out_specs=out_specs, check_vma=False
    )
```

```python
import jax
import jax.numpy as jnp
import numpy as np
from jax import lax
from jax.experimental import pallas as pl
from jax.experimental.pallas import tpu as pltpu
from jax.sharding import PartitionSpec as P

leak_slope = 0.2
same_core = [list(range(0, 16, 2)), list(range(1, 16, 2))]
mib = 1024 * 1024


def partners(first, last):
    low = lax.axis_index("sx") % 2 == 0
    near = lax.ppermute(jnp.where(low, last, first), "sx", [(i, i ^ 1) for i in range(16)])
    far = lax.ppermute(
        jnp.where(low, first, last), "sx", [(i, i - 1 + 2 * (i % 2)) for i in range(1, 15)]
    )
    return near, far


def neighbours(first, last, axis):
    ends = lax.axis_size(axis) - 1
    return (
        lax.ppermute(last, axis, [(i, i + 1) for i in range(ends)]),
        lax.ppermute(first, axis, [(i + 1, i) for i in range(ends)]),
    )


def other_core(values):
    return lax.ppermute(values, "sx", [(i, i ^ 1) for i in range(16)])


def to_chips(parts):
    return lax.all_to_all(parts, "sx", 0, 0, axis_index_groups=same_core, tiled=True)


def to_sy(parts):
    return lax.all_to_all(parts, "sy", 0, 0, tiled=True)


def repeated(part, count):
    return jnp.broadcast_to(part[None], (count,) + part.shape)


def sum_first(parts):
    return parts.astype(jnp.float32).sum(0)


def dot(left, right):
    return jnp.dot(left, right, preferred_element_type=jnp.float32)


def row_before(values):
    rows = lax.broadcasted_iota(jnp.int32, values.shape, 0)
    return jnp.where(rows == 0, 0.0, pltpu.roll(values, 1, 0))


def row_after(values):
    count = values.shape[0]
    rows = lax.broadcasted_iota(jnp.int32, values.shape, 0)
    return jnp.where(rows == count - 1, 0.0, pltpu.roll(values, count - 1, 0))


def call(body, outs, scratch, operands, vmem, smem=0, flops=0, name=None):
    size = sum(int(np.prod(a.shape)) * a.dtype.itemsize for a in operands)
    size += sum(int(np.prod(shape)) * jnp.dtype(kind).itemsize for shape, kind in outs)
    whole = pl.BlockSpec(memory_space=pltpu.VMEM)
    specs = [whole] * (len(operands) - smem) + [pl.BlockSpec(memory_space=pltpu.SMEM)] * smem
    return pl.pallas_call(
        body,
        out_shape=[jax.ShapeDtypeStruct(shape, kind) for shape, kind in outs],
        in_specs=specs,
        out_specs=[whole] * len(outs),
        scratch_shapes=[pltpu.VMEM(shape, kind) for shape, kind in scratch],
        compiler_params=pltpu.CompilerParams(vmem_limit_bytes=vmem * mib),
        cost_estimate=pl.CostEstimate(flops=flops, bytes_accessed=size, transcendentals=0),
        name=name,
    )(*operands)


def pair_select():
    sel = np.zeros((256, 4, 128), np.float32)
    for k, offset in enumerate((0, 1, -1, 2)):
        for p in range(128):
            if 0 <= 2 * p + offset < 256:
                sel[2 * p + offset, k, p] = 1
    return jnp.asarray(sel.reshape(256, 512), jnp.bfloat16)


def pair_filters(kernel):
    taps = kernel.reshape(9, 3, 64, 128)
    none = jnp.zeros((9, 64, 128), kernel.dtype)
    even = jnp.concatenate([taps[:, 1], taps[:, 2], taps[:, 0], none], axis=1)
    odd = jnp.concatenate([taps[:, 0], taps[:, 1], none, taps[:, 2]], axis=1)
    return jnp.concatenate([even, odd], axis=2)


def first_body(vc, vzl, vzh, vyl, vyh, w1, sel, pooled, bits, xt, xc, acc):
    for z in range(6):
        rows = vzl[0] if z == 0 else vzh[0] if z == 5 else vc[z - 1]
        got = dot(rows.reshape(512, 256), sel[...]).astype(jnp.bfloat16)
        low = dot(vyl[z, 0], sel[...]).astype(jnp.bfloat16)
        high = dot(vyh[z, 0], sel[...]).astype(jnp.bfloat16)
        for k in range(4):
            lanes = slice(k * 128, k * 128 + 128)
            place = slice(k * 64, k * 64 + 64)
            xt[z, place, 0:128] = low[:, lanes]
            xt[z, place, 1152:1280] = high[:, lanes]
            for y in range(8):
                xt[z, place, (y + 1) * 128 : (y + 2) * 128] = got[y * 64 : y * 64 + 64, lanes]
        xc[z] = xt[z].T

    @pl.loop(0, 2)
    def _(zp):
        for zz in range(2):
            total = None
            for a in range(3):
                for b in range(3):
                    part = dot(xc[2 * zp + zz + a, b * 128 : b * 128 + 1024, :], w1[3 * a + b])
                    total = part if total is None else total + part
            acc[zz] = total
        for yp in range(4):
            mean = jnp.zeros((128, 128), jnp.float32)
            mask = jnp.zeros((128, 128), jnp.int32)
            for zz in range(2):
                for yy in range(2):
                    for par in range(2):
                        row = (2 * yp + yy) * 128
                        v = acc[zz, row : row + 128, par * 128 : par * 128 + 128]
                        up = v > 0
                        mean += jnp.where(up, v, leak_slope * v)
                        mask |= jnp.where(up, 1 << (zz * 4 + yy * 2 + par), 0)
            pooled[zp, yp] = (mean * 0.125).astype(jnp.bfloat16)
            bits[zp, yp] = mask


def first_section(vc, vzl, vzh, vyl, vyh, w1):
    return call(
        first_body,
        [
            ((2, 4, 128, 128), jnp.bfloat16),
            ((2, 4, 128, 128), jnp.int32),
            ((6, 256, 1280), jnp.bfloat16),
        ],
        [((6, 1280, 256), jnp.bfloat16), ((2, 1024, 256), jnp.float32)],
        [vc, vzl, vzh, vyl, vyh, w1, pair_select()],
        flops=5_000_000_000,
        vmem=18,
        name="first",
    )


def lay_filters(place, tap_of, turn):
    for b in range(3):
        for four in range(4):
            for c in range(3):
                for two in range(2):
                    a = four - two
                    lanes = slice(c * 256 + two * 128, c * 256 + two * 128 + 128)
                    block = (b, slice(four * 128, four * 128 + 128), lanes)
                    if 0 <= a < 3:
                        tap = tap_of(a, b, c)
                        place[block] = tap.T if turn else tap
                    else:
                        place[block] = jnp.zeros((128, 128), jnp.bfloat16)


def conv_rows(source, lanes, filters, total, count):
    rows = count * 128
    parts = None
    for b in range(3):
        part = dot(source[b : b + count, :, lanes].reshape(rows, 512), filters[b])
        parts = part if parts is None else parts + part
    total[0:rows, :] = parts


def joined(total, y):
    rows = slice(y * 128, y * 128 + 128)
    return (
        row_before(total[rows, 0:256]) + total[rows, 256:512] + row_after(total[rows, 512:768])
    )


def cot_body(half, near, k3, core, hidden_grad, cot3, cells, filters, total):
    first = core[0] * 2
    for z in range(4):
        for y in range(8):
            lanes = pl.ds(pl.multiple_of((first + z) * 128, 128), 128)
            cells[y, :, lanes] = half[z, y].T
    for z in range(2):
        for y in range(8):
            lanes = pl.ds(pl.multiple_of((4 - 2 * first + z) * 128, 128), 128)
            cells[y, :, lanes] = near[z, y].T
    lay_filters(filters, lambda a, b, c: k3[(2 - a) * 9 + (2 - b) * 3 + 2 - c], True)
    for j in range(2):
        conv_rows(cells, slice(j * 256, j * 256 + 512), filters, total, 6)
        for y in range(6):
            hidden_grad[y, :, j * 256 : j * 256 + 256] = joined(total, y)
    for y in range(4):
        own = cells[y + 2, :, 256:512].astype(jnp.float32)
        rows = slice(y * 128, y * 128 + 128)
        cot3[rows, 0:256] = row_after(own).astype(jnp.bfloat16)
        cot3[rows, 256:512] = own.astype(jnp.bfloat16)
        cot3[rows, 512:768] = row_before(own).astype(jnp.bfloat16)


def cot_section(half, near, core, k3):
    return call(
        cot_body,
        [((6, 128, 512), jnp.float32), ((512, 768), jnp.bfloat16)],
        [
            ((8, 128, 768), jnp.bfloat16),
            ((3, 512, 768), jnp.bfloat16),
            ((768, 768), jnp.float32),
        ],
        [half, near, k3, core.reshape(1)],
        smem=1,
        flops=3_600_000_000,
        vmem=16,
        name="cot",
    )


def grad_taps(turned, cot3, store):
    for b in range(3):
        full = dot(turned[:, b * 128 : b * 128 + 512], cot3[...])
        for a in range(3):
            for c in range(3):
                low = full[a * 128 : a * 128 + 128, c * 256 : c * 256 + 128]
                high = full[a * 128 + 128 : a * 128 + 256, c * 256 + 128 : c * 256 + 256]
                store(9 * a + 3 * b + c, low + high)


def mid_body(
    own, near, far, ends, near_ends, far_ends, hidden_grad, cot3, k2, k3, flags, core,
    maps, spg, cells, hidden, filters, total, spg3, turned,
):
    at_near = 512 - 512 * core[0]
    for z in range(2):
        for part, part_ends, at in (
            (own, ends, None),
            (near, near_ends, at_near + z * 128),
            (far, far_ends, 512 - at_near + z * 128),
        ):
            lanes = (
                slice(256 + z * 128, 384 + z * 128)
                if at is None
                else pl.ds(pl.multiple_of(at, 128), 128)
            )
            for y in range(2):
                cells[y, :, lanes] = part_ends[z, y]
                cells[y + 6, :, lanes] = part_ends[z, y + 2]
            for y in range(4):
                cells[y + 2, :, lanes] = part[z, y]
    lay_filters(filters, lambda a, b, c: k2[9 * a + 3 * b + c], True)
    lane = lax.broadcasted_iota(jnp.int32, (128, 256), 1)
    for j in range(2):
        conv_rows(cells, slice(j * 256, j * 256 + 512), filters, total, 6)
        edge = lane < 128 if j == 0 else lane >= 128
        inside = jnp.where(edge, flags[j], 1.0)
        for y in range(6):
            pre = joined(total, y)
            keep = inside * flags[2] if y == 0 else inside * flags[3] if y == 5 else inside
            lanes = slice(j * 256, j * 256 + 256)
            up = pre > 0
            hidden[y, :, lanes] = (jnp.where(up, pre, leak_slope * pre) * keep).astype(
                jnp.bfloat16
            )
            back = hidden_grad[y, :, lanes]
            spg[y, :, lanes] = (jnp.where(up, back, leak_slope * back) * keep).astype(
                jnp.bfloat16
            )
    turned[...] = hidden[...].reshape(768, 512).T

    def store(place, value):
        for i in range(16):
            maps[(i + core[0]) % 2, i // 2, place] = value[i * 8 : i * 8 + 8]

    def store_third(tap, value):
        store(27 + tap, value)

    grad_taps(turned, cot3, store_third)
    store(54, jnp.zeros((128, 128), jnp.float32))
    store(55, jnp.zeros((128, 128), jnp.float32))
    for y in range(4):
        own = spg[y + 1, :, 128:384].astype(jnp.float32)
        rows = slice(y * 128, y * 128 + 128)
        spg3[rows, 0:256] = row_after(own).astype(jnp.bfloat16)
        spg3[rows, 256:512] = own.astype(jnp.bfloat16)
        spg3[rows, 512:768] = row_before(own).astype(jnp.bfloat16)
    turned[...] = cells[1:7, :, 128:640].reshape(768, 512).T

    def store_second(tap, value):
        store(tap, value.T)

    grad_taps(turned, spg3, store_second)
    lay_filters(filters, lambda a, b, c: k3[9 * a + 3 * b + c], False)
    conv_rows(hidden, slice(0, 512), filters, total, 4)
    for y in range(4):
        done = joined(total, y)
        for z in range(2):
            store(56 + z * 4 + y, done[:, z * 128 : z * 128 + 128].T)


def mid_section(
    own, near, far, ends, near_ends, far_ends, hidden_grad, cot3, k2, k3, flags, core
):
    return call(
        mid_body,
        [
            ((2, 8, 64, 8, 128), jnp.float32),
            ((6, 128, 512), jnp.bfloat16),
        ],
        [
            ((8, 128, 768), jnp.bfloat16),
            ((6, 128, 512), jnp.bfloat16),
            ((3, 512, 768), jnp.bfloat16),
            ((768, 768), jnp.float32),
            ((512, 768), jnp.bfloat16),
            ((512, 768), jnp.bfloat16),
        ],
        [own, near, far, ends, near_ends, far_ends, hidden_grad, cot3, k2, k3]
        + [flags, core.reshape(1)],
        smem=2,
        flops=7_000_000_000,
        vmem=26,
        name="mid",
    )


def last_body(spg, k2, xt, bits, core, first, filters, total, back, full):
    lay_filters(filters, lambda a, b, c: k2[(2 - a) * 9 + (2 - b) * 3 + 2 - c], False)
    conv_rows(spg, slice(0, 512), filters, total, 4)
    for y in range(4):
        grad = joined(total, y).astype(jnp.bfloat16).astype(jnp.float32)
        for z in range(2):
            share = grad[:, z * 128 : z * 128 + 128] * 0.125
            up, down = share.astype(jnp.bfloat16), (share * leak_slope).astype(jnp.bfloat16)
            up, down = up.astype(jnp.float32), down.astype(jnp.float32)
            mask = bits[z, y]
            for zz in range(2):
                for yy in range(2):
                    for par in range(2):
                        bit = mask & (1 << (zz * 4 + yy * 2 + par))
                        row = (2 * y + yy) * 128
                        back[2 * z + zz, row : row + 128, par * 128 : par * 128 + 128] = (
                            jnp.where(bit != 0, up, down).astype(jnp.bfloat16)
                        )
    for b in range(3):
        parts = None
        for z in range(4):
            left = xt[z : z + 3, :, b * 128 : b * 128 + 1024].reshape(768, 1024)
            part = dot(left, back[z])
            parts = part if parts is None else parts + part
        full[...] = parts
        for a in range(3):
            for c in range(3):
                even, odd = ((2, 0), (0, 1), (1, 3))[c]
                low = full[a * 256 + even * 64 : a * 256 + even * 64 + 64, 0:128]
                high = full[a * 256 + odd * 64 : a * 256 + odd * 64 + 64, 128:256]
                tap = 9 * a + 3 * b + c
                row = tap // 4 * 128 + tap % 2 * 64
                first[(tap // 2 + core[0]) % 2, row : row + 64, :] = low + high
    first[core[0], 896:1024, :] = jnp.zeros((128, 128), jnp.float32)
    first[1 - core[0], 832:1024, :] = jnp.zeros((192, 128), jnp.float32)


def last_section(spg, k2, xt, bits, core):
    return call(
        last_body,
        [((2, 1024, 128), jnp.float32)],
        [
            ((3, 512, 768), jnp.bfloat16),
            ((768, 768), jnp.float32),
            ((4, 1024, 256), jnp.bfloat16),
            ((768, 256), jnp.float32),
        ],
        [spg, k2, xt, bits, core.reshape(1)],
        smem=1,
        flops=6_000_000_000,
        vmem=20,
        name="last",
    )[0]


def cot_rows(values):
    own = values.reshape(4, 8, 4, 8, 128)
    below = jnp.pad(own[:, :7, 2:], ((0, 0), (1, 0), (0, 0), (0, 0), (0, 0)))
    above = jnp.pad(own[:, 1:, :2], ((0, 0), (0, 1), (0, 0), (0, 0), (0, 0)))
    return jnp.swapaxes(jnp.concatenate([below, own, above], axis=2), 0, 1)


def cot_deep(values):
    wide = jnp.pad(values.reshape(32, 8, 8, 128), ((2, 2), (0, 0), (0, 0), (0, 0)))
    wide = wide.reshape(9, 4, 8, 8, 128)
    return jnp.stack([wide[:8], wide[1:]], axis=1).reshape(16, 4, 8, 8, 128)


def after(values, *done):
    return lax.optimization_barrier((values,) + done)[0]


def on_device(volume, first_kernel, second_kernel, third_kernel, cotangent):
    sx, sy = lax.axis_index("sx"), lax.axis_index("sy")
    core = sx % 2
    flags = jnp.stack([sx > 0, sx < 15, sy > 0, sy < 7]).astype(jnp.float32)
    shares = jnp.concatenate(
        [jnp.swapaxes(second_kernel, 3, 4).reshape(216, 128), third_kernel.reshape(216, 128)]
    )
    filters = lax.all_gather(shares, "sx", axis=0, tiled=True)
    vc = jnp.swapaxes(volume, 2, 3)
    near, far = partners(after(vc[:1], shares), vc[-1:])
    vzl, vzh = jnp.where(core == 0, far, near), jnp.where(core == 0, near, far)
    deep = lambda y: jnp.concatenate([vzl[:, y : y + 1], vc[:, y : y + 1], vzh[:, y : y + 1]])
    vyl, vyh = neighbours(deep(0), deep(7), "sy")
    cot_tall = to_sy(after(cot_rows(jnp.swapaxes(cotangent, 2, 3)), near))
    cot_parts = lax.all_to_all(cot_deep(cot_tall), "sx", 0, 0, tiled=True)
    cot_half = cot_parts.transpose(1, 2, 0, 3, 4).reshape(4, 8, 128, 128)
    cot_near = other_core(jnp.where(core == 0, cot_half[2:], cot_half[:2]))
    w1 = after(pair_filters(first_kernel), cot_tall)
    pooled, bits, xt = first_section(vc, vzl, vzh, vyl, vyh, w1)
    pyl, pyh = neighbours(pooled[:, :2], pooled[:, 2:], "sy")
    near, far = partners(pooled, pooled)
    ends = jnp.concatenate([pyl, pyh], axis=1)
    near_ends, far_ends = partners(ends, ends)
    filters = filters.reshape(16, 54, 8, 128).swapaxes(0, 1).reshape(54, 128, 128)
    k2, k3 = filters[:27], filters[27:]
    hidden_grad, cot3 = cot_section(cot_half, cot_near, core, k3)
    maps, spg = mid_section(
        pooled, near, far, ends, near_ends, far_ends, hidden_grad, cot3, k2, k3, flags, core
    )
    from_other = other_core(maps[1].astype(jnp.bfloat16))
    own = maps[0]
    mine, theirs = own[:, 56:].astype(jnp.bfloat16), from_other[:, 56:]
    first_part = last_section(spg, k2, xt, bits, core)
    first_from = other_core(first_part[1].astype(jnp.bfloat16))
    first_half = first_part[0] + first_from.astype(jnp.float32)
    grads = own[:, :56] + from_other[:, :56].astype(jnp.float32)
    parts = jnp.concatenate(
        [
            grads.astype(jnp.bfloat16),
            jnp.where(core == 0, mine, theirs),
            jnp.where(core == 0, theirs, mine),
            first_half.astype(jnp.bfloat16).reshape(8, 16, 8, 128),
        ],
        axis=1,
    )
    parts = to_chips(parts)
    parts = jnp.concatenate(
        [
            sum_first(parts[:, :56]).astype(jnp.bfloat16).reshape(8, 7, 8, 128),
            sum_first(parts[:, 72:]).astype(jnp.bfloat16).reshape(8, 2, 8, 128),
            parts[:, 56:72],
        ],
        axis=1,
    )
    parts = to_sy(parts)
    output = parts[:, 9:].reshape(8, 4, 4, 8, 128).swapaxes(0, 1).reshape(4, 32, 8, 128)
    share = to_sy(repeated(sum_first(parts[:, :9]).astype(jnp.bfloat16), 8))
    grads = share[:, :7].reshape(56, 8, 128)[:54].astype(jnp.float32)
    grads = grads.reshape(2, 3, 3, 3, 8, 128)
    first_grad = repeated(share[:, 7:].reshape(128, 128), 16)
    first_grad = lax.all_to_all(first_grad, "sx", 0, 0, tiled=True).reshape(2048, 128)[:1728]
    first_grad = first_grad.astype(jnp.float32).reshape(3, 3, 3, 64, 128)
    return (jnp.swapaxes(output, 2, 3), first_grad, jnp.swapaxes(grads[0], 3, 4), grads[1])


def solution(mesh):
    in_specs = (
        P("sx", "sy", None, None),
        P(),
        P(None, None, None, None, "sx"),
        P(None, None, None, "sx", None),
        P("sy", None, None, "sx"),
    )
    out_specs = (
        P("sy", None, None, "sx"),
        P(),
        P(None, None, None, None, "sx"),
        P(None, None, None, "sx", None),
    )
    return jax.shard_map(
        on_device, mesh=mesh, in_specs=in_specs, out_specs=out_specs, check_vma=False
    )
```

```python
import jax
import jax.numpy as jnp
import numpy as np
from jax import lax
from jax.experimental import pallas as pl
from jax.experimental.pallas import tpu as pltpu
from jax.sharding import PartitionSpec as P

leak_slope = 0.2
same_core = [list(range(0, 16, 2)), list(range(1, 16, 2))]
mib = 1024 * 1024


def partners(first, last, tie=None):
    low = lax.axis_index("sx") % 2 == 0
    to_near, to_far = jnp.where(low, last, first), jnp.where(low, first, last)
    if tie is not None:
        to_near, to_far = after(to_near, tie), after(to_far, tie)
    near = lax.ppermute(to_near, "sx", [(i, i ^ 1) for i in range(16)])
    far = lax.ppermute(to_far, "sx", [(i, i - 1 + 2 * (i % 2)) for i in range(1, 15)])
    return near, far


def neighbours(first, last, axis):
    ends = lax.axis_size(axis) - 1
    return (
        lax.ppermute(last, axis, [(i, i + 1) for i in range(ends)]),
        lax.ppermute(first, axis, [(i + 1, i) for i in range(ends)]),
    )


def other_core(values):
    return lax.ppermute(values, "sx", [(i, i ^ 1) for i in range(16)])


def to_chips(parts):
    return lax.all_to_all(parts, "sx", 0, 0, axis_index_groups=same_core, tiled=True)


def to_sy(parts):
    return lax.all_to_all(parts, "sy", 0, 0, tiled=True)


def repeated(part, count):
    return jnp.broadcast_to(part[None], (count,) + part.shape)


def sum_first(parts):
    return parts.astype(jnp.float32).sum(0)


def dot(left, right):
    return jnp.dot(left, right, preferred_element_type=jnp.float32)


def row_before(values):
    rows = lax.broadcasted_iota(jnp.int32, values.shape, 0)
    return jnp.where(rows == 0, 0.0, pltpu.roll(values, 1, 0))


def row_after(values):
    count = values.shape[0]
    rows = lax.broadcasted_iota(jnp.int32, values.shape, 0)
    return jnp.where(rows == count - 1, 0.0, pltpu.roll(values, count - 1, 0))


def call(body, outs, scratch, operands, vmem, smem=0, flops=0, name=None):
    size = sum(int(np.prod(a.shape)) * a.dtype.itemsize for a in operands)
    size += sum(int(np.prod(shape)) * jnp.dtype(kind).itemsize for shape, kind in outs)
    whole = pl.BlockSpec(memory_space=pltpu.VMEM)
    specs = [whole] * (len(operands) - smem) + [pl.BlockSpec(memory_space=pltpu.SMEM)] * smem
    return pl.pallas_call(
        body,
        out_shape=[jax.ShapeDtypeStruct(shape, kind) for shape, kind in outs],
        in_specs=specs,
        out_specs=[whole] * len(outs),
        scratch_shapes=[pltpu.VMEM(shape, kind) for shape, kind in scratch],
        compiler_params=pltpu.CompilerParams(vmem_limit_bytes=vmem * mib),
        cost_estimate=pl.CostEstimate(flops=flops, bytes_accessed=size, transcendentals=0),
        name=name,
    )(*operands)


def pair_select():
    sel = np.zeros((256, 4, 128), np.float32)
    for k, offset in enumerate((0, 1, -1, 2)):
        for p in range(128):
            if 0 <= 2 * p + offset < 256:
                sel[2 * p + offset, k, p] = 1
    return jnp.asarray(sel.reshape(256, 512), jnp.bfloat16)


def pair_filters(kernel):
    taps = kernel.reshape(9, 3, 64, 128)
    none = jnp.zeros((9, 64, 128), kernel.dtype)
    even = jnp.concatenate([taps[:, 1], taps[:, 2], taps[:, 0], none], axis=1)
    odd = jnp.concatenate([taps[:, 0], taps[:, 1], none, taps[:, 2]], axis=1)
    return jnp.concatenate([even, odd], axis=2)


def first_body(vc, vzl, vzh, vyl, vyh, w1, sel, pooled, xt, xc, acc):
    for z in range(6):
        rows = vzl[0] if z == 0 else vzh[0] if z == 5 else vc[z - 1]
        got = dot(rows.reshape(512, 256), sel[...]).astype(jnp.bfloat16)
        low = dot(vyl[z, 0], sel[...]).astype(jnp.bfloat16)
        high = dot(vyh[z, 0], sel[...]).astype(jnp.bfloat16)
        for k in range(4):
            lanes = slice(k * 128, k * 128 + 128)
            place = slice(k * 64, k * 64 + 64)
            xt[z, place, 0:128] = low[:, lanes]
            xt[z, place, 1152:1280] = high[:, lanes]
            for y in range(8):
                xt[z, place, (y + 1) * 128 : (y + 2) * 128] = got[y * 64 : y * 64 + 64, lanes]
        xc[z] = xt[z].T

    @pl.loop(0, 2)
    def _(zp):
        for zz in range(2):
            total = None
            for a in range(3):
                for b in range(3):
                    part = dot(xc[2 * zp + zz + a, b * 128 : b * 128 + 1024, :], w1[3 * a + b])
                    total = part if total is None else total + part
            acc[zz] = total
        for yp in range(4):
            mean = jnp.zeros((128, 128), jnp.float32)
            mask = jnp.zeros((128, 128), jnp.int32)
            for zz in range(2):
                for yy in range(2):
                    for par in range(2):
                        row = (2 * yp + yy) * 128
                        v = acc[zz, row : row + 128, par * 128 : par * 128 + 128]
                        up = v > 0
                        mean += jnp.where(up, v, leak_slope * v)
                        mask |= jnp.where(up, 1 << (zz * 4 + yy * 2 + par), 0)
            pooled[zp, yp] = (mean * 0.125).astype(jnp.bfloat16)
            lanes = slice(yp * 128, yp * 128 + 128)
            rows = pl.ds(pl.multiple_of(zp * 128, 128), 128)
            xt[6, rows, lanes] = mask.astype(jnp.float32).astype(jnp.bfloat16)


def first_section(vc, vzl, vzh, vyl, vyh, w1):
    return call(
        first_body,
        [
            ((2, 4, 128, 128), jnp.bfloat16),
            ((7, 256, 1280), jnp.bfloat16),
        ],
        [((6, 1280, 256), jnp.bfloat16), ((2, 1024, 256), jnp.float32)],
        [vc, vzl, vzh, vyl, vyh, w1, pair_select()],
        flops=5_000_000_000,
        vmem=18,
        name="first",
    )


def lay_filters(place, tap_of, turn):
    for b in range(3):
        for four in range(4):
            for c in range(3):
                for two in range(2):
                    a = four - two
                    lanes = slice(c * 256 + two * 128, c * 256 + two * 128 + 128)
                    block = (b, slice(four * 128, four * 128 + 128), lanes)
                    if 0 <= a < 3:
                        tap = tap_of(a, b, c)
                        place[block] = tap.T if turn else tap
                    else:
                        place[block] = jnp.zeros((128, 128), jnp.bfloat16)


def conv_rows(source, lanes, filters, total, count):
    rows = count * 128
    parts = None
    for b in range(3):
        part = dot(source[b : b + count, :, lanes].reshape(rows, 512), filters[b])
        parts = part if parts is None else parts + part
    total[0:rows, :] = parts


def joined(total, y):
    rows = slice(y * 128, y * 128 + 128)
    return (
        row_before(total[rows, 0:256]) + total[rows, 256:512] + row_after(total[rows, 512:768])
    )


def cot_body(half, near, k3, core, hidden_grad, cot3, cells, filters, total):
    first = core[0] * 2
    for z in range(4):
        for y in range(8):
            lanes = pl.ds(pl.multiple_of((first + z) * 128, 128), 128)
            cells[y, :, lanes] = half[z, y].T
    for z in range(2):
        for y in range(8):
            lanes = pl.ds(pl.multiple_of((4 - 2 * first + z) * 128, 128), 128)
            cells[y, :, lanes] = near[z, y].T
    lay_filters(filters, lambda a, b, c: k3[(2 - a) * 9 + (2 - b) * 3 + 2 - c], True)
    for j in range(2):
        conv_rows(cells, slice(j * 256, j * 256 + 512), filters, total, 6)
        for y in range(6):
            hidden_grad[y, :, j * 256 : j * 256 + 256] = joined(total, y)
    for y in range(4):
        own = cells[y + 2, :, 256:512].astype(jnp.float32)
        rows = slice(y * 128, y * 128 + 128)
        cot3[rows, 0:256] = row_after(own).astype(jnp.bfloat16)
        cot3[rows, 256:512] = own.astype(jnp.bfloat16)
        cot3[rows, 512:768] = row_before(own).astype(jnp.bfloat16)


def cot_section(half, near, core, k3):
    return call(
        cot_body,
        [((6, 128, 512), jnp.float32), ((512, 768), jnp.bfloat16)],
        [
            ((8, 128, 768), jnp.bfloat16),
            ((3, 512, 768), jnp.bfloat16),
            ((768, 768), jnp.float32),
        ],
        [half, near, k3, core.reshape(1)],
        smem=1,
        flops=3_600_000_000,
        vmem=16,
        name="cot",
    )


def grad_taps(turned, cot3, store):
    for b in range(3):
        full = dot(turned[:, b * 128 : b * 128 + 512], cot3[...])
        for a in range(3):
            for c in range(3):
                low = full[a * 128 : a * 128 + 128, c * 256 : c * 256 + 128]
                high = full[a * 128 + 128 : a * 128 + 256, c * 256 + 128 : c * 256 + 256]
                store(9 * a + 3 * b + c, low + high)


def mid_body(
    own, near, far, ends, near_ends, far_ends, hidden_grad, cot3, k2, k3, flags, core,
    maps, spg, cells, hidden, filters, total, spg3, turned,
):
    at_near = 512 - 512 * core[0]
    for z in range(2):
        for part, part_ends, at in (
            (own, ends, None),
            (near, near_ends, at_near + z * 128),
            (far, far_ends, 512 - at_near + z * 128),
        ):
            lanes = (
                slice(256 + z * 128, 384 + z * 128)
                if at is None
                else pl.ds(pl.multiple_of(at, 128), 128)
            )
            for y in range(2):
                cells[y, :, lanes] = part_ends[z, y]
                cells[y + 6, :, lanes] = part_ends[z, y + 2]
            for y in range(4):
                cells[y + 2, :, lanes] = part[z, y]
    lay_filters(filters, lambda a, b, c: k2[9 * a + 3 * b + c], True)
    lane = lax.broadcasted_iota(jnp.int32, (128, 256), 1)
    for j in range(2):
        conv_rows(cells, slice(j * 256, j * 256 + 512), filters, total, 6)
        edge = lane < 128 if j == 0 else lane >= 128
        inside = jnp.where(edge, flags[j], 1.0)
        for y in range(6):
            pre = joined(total, y)
            keep = inside * flags[2] if y == 0 else inside * flags[3] if y == 5 else inside
            lanes = slice(j * 256, j * 256 + 256)
            up = pre > 0
            hidden[y, :, lanes] = (jnp.where(up, pre, leak_slope * pre) * keep).astype(
                jnp.bfloat16
            )
            back = hidden_grad[y, :, lanes]
            spg[y, :, lanes] = (jnp.where(up, back, leak_slope * back) * keep).astype(
                jnp.bfloat16
            )
    turned[...] = hidden[...].reshape(768, 512).T

    def store(place, value):
        for i in range(16):
            maps[(i + core[0]) % 2, i // 2, place] = value[i * 8 : i * 8 + 8]

    def store_third(tap, value):
        store(27 + tap, value)

    grad_taps(turned, cot3, store_third)
    store(54, jnp.zeros((128, 128), jnp.float32))
    store(55, jnp.zeros((128, 128), jnp.float32))
    for y in range(4):
        own = spg[y + 1, :, 128:384].astype(jnp.float32)
        rows = slice(y * 128, y * 128 + 128)
        spg3[rows, 0:256] = row_after(own).astype(jnp.bfloat16)
        spg3[rows, 256:512] = own.astype(jnp.bfloat16)
        spg3[rows, 512:768] = row_before(own).astype(jnp.bfloat16)
    turned[...] = cells[1:7, :, 128:640].reshape(768, 512).T

    def store_second(tap, value):
        store(tap, value.T)

    grad_taps(turned, spg3, store_second)
    lay_filters(filters, lambda a, b, c: k3[9 * a + 3 * b + c], False)
    conv_rows(hidden, slice(0, 512), filters, total, 4)
    for y in range(4):
        done = joined(total, y)
        for z in range(2):
            store(56 + z * 4 + y, done[:, z * 128 : z * 128 + 128].T)


def mid_section(
    own, near, far, ends, near_ends, far_ends, hidden_grad, cot3, k2, k3, flags, core
):
    return call(
        mid_body,
        [
            ((2, 8, 64, 8, 128), jnp.float32),
            ((6, 128, 512), jnp.bfloat16),
        ],
        [
            ((8, 128, 768), jnp.bfloat16),
            ((6, 128, 512), jnp.bfloat16),
            ((3, 512, 768), jnp.bfloat16),
            ((768, 768), jnp.float32),
            ((512, 768), jnp.bfloat16),
            ((512, 768), jnp.bfloat16),
        ],
        [own, near, far, ends, near_ends, far_ends, hidden_grad, cot3, k2, k3]
        + [flags, core.reshape(1)],
        smem=2,
        flops=7_000_000_000,
        vmem=26,
        name="mid",
    )


def last_body(spg, k2, xt, core, first, filters, total, back, full):
    lay_filters(filters, lambda a, b, c: k2[(2 - a) * 9 + (2 - b) * 3 + 2 - c], False)
    conv_rows(spg, slice(0, 512), filters, total, 4)
    for y in range(4):
        grad = joined(total, y).astype(jnp.bfloat16).astype(jnp.float32)
        for z in range(2):
            share = grad[:, z * 128 : z * 128 + 128] * 0.125
            up, down = share.astype(jnp.bfloat16), (share * leak_slope).astype(jnp.bfloat16)
            up, down = up.astype(jnp.float32), down.astype(jnp.float32)
            mask = xt[6, z * 128 : z * 128 + 128, y * 128 : y * 128 + 128]
            mask = mask.astype(jnp.float32).astype(jnp.int32)
            for zz in range(2):
                for yy in range(2):
                    for par in range(2):
                        bit = mask & (1 << (zz * 4 + yy * 2 + par))
                        row = (2 * y + yy) * 128
                        back[2 * z + zz, row : row + 128, par * 128 : par * 128 + 128] = (
                            jnp.where(bit != 0, up, down).astype(jnp.bfloat16)
                        )
    for b in range(3):
        parts = None
        for z in range(4):
            left = xt[z : z + 3, :, b * 128 : b * 128 + 1024].reshape(768, 1024)
            part = dot(left, back[z])
            parts = part if parts is None else parts + part
        full[...] = parts
        for a in range(3):
            for c in range(3):
                even, odd = ((2, 0), (0, 1), (1, 3))[c]
                low = full[a * 256 + even * 64 : a * 256 + even * 64 + 64, 0:128]
                high = full[a * 256 + odd * 64 : a * 256 + odd * 64 + 64, 128:256]
                tap = 9 * a + 3 * b + c
                row = tap // 4 * 128 + tap % 2 * 64
                first[(tap // 2 + core[0]) % 2, row : row + 64, :] = low + high
    first[core[0], 896:1024, :] = jnp.zeros((128, 128), jnp.float32)
    first[1 - core[0], 832:1024, :] = jnp.zeros((192, 128), jnp.float32)


def last_section(spg, k2, xt, core):
    return call(
        last_body,
        [((2, 1024, 128), jnp.float32)],
        [
            ((3, 512, 768), jnp.bfloat16),
            ((768, 768), jnp.float32),
            ((4, 1024, 256), jnp.bfloat16),
            ((768, 256), jnp.float32),
        ],
        [spg, k2, xt, core.reshape(1)],
        smem=1,
        flops=6_000_000_000,
        vmem=20,
        name="last",
    )[0]


def cot_rows(values):
    own = values.reshape(4, 8, 4, 8, 128)
    below = jnp.pad(own[:, :7, 2:], ((0, 0), (1, 0), (0, 0), (0, 0), (0, 0)))
    above = jnp.pad(own[:, 1:, :2], ((0, 0), (0, 1), (0, 0), (0, 0), (0, 0)))
    return jnp.swapaxes(jnp.concatenate([below, own, above], axis=2), 0, 1)


def cot_deep(values):
    wide = jnp.pad(values.reshape(32, 8, 8, 128), ((2, 2), (0, 0), (0, 0), (0, 0)))
    wide = wide.reshape(9, 4, 8, 8, 128)
    return jnp.stack([wide[:8], wide[1:]], axis=1).reshape(16, 4, 8, 8, 128)


def after(values, *done):
    return lax.optimization_barrier((values,) + done)[0]


def on_device(volume, first_kernel, second_kernel, third_kernel, cotangent):
    sx, sy = lax.axis_index("sx"), lax.axis_index("sy")
    core = sx % 2
    flags = jnp.stack([sx > 0, sx < 15, sy > 0, sy < 7]).astype(jnp.float32)
    shares = jnp.concatenate(
        [jnp.swapaxes(second_kernel, 3, 4).reshape(216, 128), third_kernel.reshape(216, 128)]
    )
    filters = lax.all_gather(shares, "sx", axis=0, tiled=True)
    vc = jnp.swapaxes(volume, 2, 3)
    near, far = partners(vc[:1], vc[-1:], shares)
    vzl, vzh = jnp.where(core == 0, far, near), jnp.where(core == 0, near, far)
    deep = lambda y: jnp.concatenate([vzl[:, y : y + 1], vc[:, y : y + 1], vzh[:, y : y + 1]])
    vyl, vyh = neighbours(deep(0), deep(7), "sy")
    cot_tall = to_sy(after(cot_rows(jnp.swapaxes(cotangent, 2, 3)), near))
    cot_parts = lax.all_to_all(cot_deep(cot_tall), "sx", 0, 0, tiled=True)
    cot_half = cot_parts.transpose(1, 2, 0, 3, 4).reshape(4, 8, 128, 128)
    cot_half = lax.optimization_barrier(cot_half)
    cot_near = other_core(jnp.where(core == 0, cot_half[2:], cot_half[:2]))
    w1 = after(pair_filters(first_kernel), cot_tall)
    pooled, xt = first_section(vc, vzl, vzh, vyl, vyh, w1)
    pyl, pyh = neighbours(pooled[:, :2], pooled[:, 2:], "sy")
    near, far = partners(pooled, pooled)
    ends = jnp.concatenate([pyl, pyh], axis=1)
    near_ends, far_ends = partners(ends, ends)
    filters = filters.reshape(16, 54, 8, 128).swapaxes(0, 1).reshape(54, 128, 128)
    k2, k3 = filters[:27], filters[27:]
    hidden_grad, cot3 = cot_section(cot_half, cot_near, core, k3)
    maps, spg = mid_section(
        pooled, near, far, ends, near_ends, far_ends, hidden_grad, cot3, k2, k3, flags, core
    )
    from_other = other_core(maps[1].astype(jnp.bfloat16))
    own = maps[0]
    mine, theirs = own[:, 56:].astype(jnp.bfloat16), from_other[:, 56:]
    first_part = last_section(spg, k2, xt, core)
    first_from = other_core(first_part[1].astype(jnp.bfloat16))
    first_half = first_part[0] + first_from.astype(jnp.float32)
    grads = own[:, :56] + from_other[:, :56].astype(jnp.float32)
    parts = jnp.concatenate(
        [
            grads.astype(jnp.bfloat16),
            jnp.where(core == 0, mine, theirs),
            jnp.where(core == 0, theirs, mine),
            first_half.astype(jnp.bfloat16).reshape(8, 16, 8, 128),
        ],
        axis=1,
    )
    parts = to_chips(parts)
    parts = jnp.concatenate(
        [
            sum_first(parts[:, :56]).astype(jnp.bfloat16).reshape(8, 7, 8, 128),
            sum_first(parts[:, 72:]).astype(jnp.bfloat16).reshape(8, 2, 8, 128),
            parts[:, 56:72],
        ],
        axis=1,
    )
    parts = to_sy(parts)
    output = parts[:, 9:].reshape(8, 4, 4, 8, 128).swapaxes(0, 1).reshape(4, 32, 8, 128)
    share = to_sy(repeated(sum_first(parts[:, :9]).astype(jnp.bfloat16), 8))
    grads = share[:, :7].reshape(56, 8, 128)[:54].astype(jnp.float32)
    grads = grads.reshape(2, 3, 3, 3, 8, 128)
    first_grad = repeated(share[:, 7:].reshape(128, 128), 16)
    first_grad = lax.all_to_all(first_grad, "sx", 0, 0, tiled=True).reshape(2048, 128)[:1728]
    first_grad = first_grad.astype(jnp.float32).reshape(3, 3, 3, 64, 128)
    return (jnp.swapaxes(output, 2, 3), first_grad, jnp.swapaxes(grads[0], 3, 4), grads[1])


def solution(mesh):
    in_specs = (
        P("sx", "sy", None, None),
        P(),
        P(None, None, None, None, "sx"),
        P(None, None, None, "sx", None),
        P("sy", None, None, "sx"),
    )
    out_specs = (
        P("sy", None, None, "sx"),
        P(),
        P(None, None, None, None, "sx"),
        P(None, None, None, "sx", None),
    )
    return jax.shard_map(
        on_device, mesh=mesh, in_specs=in_specs, out_specs=out_specs, check_vma=False
    )
```

```python
import jax
import jax.numpy as jnp
import numpy as np
from jax import lax
from jax.experimental import pallas as pl
from jax.experimental.pallas import tpu as pltpu
from jax.sharding import PartitionSpec as P

leak_slope = 0.2
same_core = [list(range(0, 16, 2)), list(range(1, 16, 2))]
mib = 1024 * 1024


def partners(first, last, tie=None):
    low = lax.axis_index("sx") % 2 == 0
    to_near, to_far = jnp.where(low, last, first), jnp.where(low, first, last)
    if tie is not None:
        to_near, to_far = after(to_near, tie), after(to_far, tie)
    near = lax.ppermute(to_near, "sx", [(i, i ^ 1) for i in range(16)])
    far = lax.ppermute(to_far, "sx", [(i, i - 1 + 2 * (i % 2)) for i in range(1, 15)])
    return near, far


def neighbours(first, last, axis):
    ends = lax.axis_size(axis) - 1
    return (
        lax.ppermute(last, axis, [(i, i + 1) for i in range(ends)]),
        lax.ppermute(first, axis, [(i + 1, i) for i in range(ends)]),
    )


def other_core(values):
    return lax.ppermute(values, "sx", [(i, i ^ 1) for i in range(16)])


def to_chips(parts):
    return lax.all_to_all(parts, "sx", 0, 0, axis_index_groups=same_core, tiled=True)


def to_sy(parts):
    return lax.all_to_all(parts, "sy", 0, 0, tiled=True)


def repeated(part, count):
    return jnp.broadcast_to(part[None], (count,) + part.shape)


def sum_first(parts):
    return parts.astype(jnp.float32).sum(0)


def dot(left, right):
    return jnp.dot(left, right, preferred_element_type=jnp.float32)


def row_before(values):
    rows = lax.broadcasted_iota(jnp.int32, values.shape, 0)
    return jnp.where(rows == 0, 0.0, pltpu.roll(values, 1, 0))


def row_after(values):
    count = values.shape[0]
    rows = lax.broadcasted_iota(jnp.int32, values.shape, 0)
    return jnp.where(rows == count - 1, 0.0, pltpu.roll(values, count - 1, 0))


def call(body, outs, scratch, operands, vmem, smem=0, flops=0, name=None):
    size = sum(int(np.prod(a.shape)) * a.dtype.itemsize for a in operands)
    size += sum(int(np.prod(shape)) * jnp.dtype(kind).itemsize for shape, kind in outs)
    whole = pl.BlockSpec(memory_space=pltpu.VMEM)
    specs = [whole] * (len(operands) - smem) + [pl.BlockSpec(memory_space=pltpu.SMEM)] * smem
    return pl.pallas_call(
        body,
        out_shape=[jax.ShapeDtypeStruct(shape, kind) for shape, kind in outs],
        in_specs=specs,
        out_specs=[whole] * len(outs),
        scratch_shapes=[pltpu.VMEM(shape, kind) for shape, kind in scratch],
        compiler_params=pltpu.CompilerParams(vmem_limit_bytes=vmem * mib),
        cost_estimate=pl.CostEstimate(flops=flops, bytes_accessed=size, transcendentals=0),
        name=name,
    )(*operands)


def pair_select():
    cell = lax.broadcasted_iota(jnp.int32, (256, 512), 0)
    lane = lax.broadcasted_iota(jnp.int32, (256, 512), 1)
    k = lane // 128
    offset = jnp.where(k == 2, -1, jnp.where(k == 3, 2, k))
    return jnp.where(cell == lane % 128 * 2 + offset, 1.0, 0.0).astype(jnp.bfloat16)


def pair_filters(kernel):
    taps = kernel.reshape(9, 3, 64, 128)
    none = jnp.zeros((9, 64, 128), kernel.dtype)
    even = jnp.concatenate([taps[:, 1], taps[:, 2], taps[:, 0], none], axis=1)
    odd = jnp.concatenate([taps[:, 0], taps[:, 1], none, taps[:, 2]], axis=1)
    return jnp.concatenate([even, odd], axis=2)


def first_body(vc, vzl, vzh, vyl, vyh, w1, pooled, xt, xc, acc, sel):
    sel[...] = pair_select()
    for z in range(6):
        rows = vzl[0] if z == 0 else vzh[0] if z == 5 else vc[z - 1]
        got = dot(rows.reshape(512, 256), sel[...]).astype(jnp.bfloat16)
        low = dot(vyl[z, 0], sel[...]).astype(jnp.bfloat16)
        high = dot(vyh[z, 0], sel[...]).astype(jnp.bfloat16)
        for k in range(4):
            lanes = slice(k * 128, k * 128 + 128)
            place = slice(k * 64, k * 64 + 64)
            xt[z, place, 0:128] = low[:, lanes]
            xt[z, place, 1152:1280] = high[:, lanes]
            for y in range(8):
                xt[z, place, (y + 1) * 128 : (y + 2) * 128] = got[y * 64 : y * 64 + 64, lanes]
        xc[z] = xt[z].T

    @pl.loop(0, 2)
    def _(zp):
        for zz in range(2):
            total = None
            for a in range(3):
                for b in range(3):
                    part = dot(xc[2 * zp + zz + a, b * 128 : b * 128 + 1024, :], w1[3 * a + b])
                    total = part if total is None else total + part
            acc[zz] = total
        for yp in range(4):
            mean = jnp.zeros((128, 128), jnp.float32)
            mask = jnp.zeros((128, 128), jnp.int32)
            for zz in range(2):
                for yy in range(2):
                    for par in range(2):
                        row = (2 * yp + yy) * 128
                        v = acc[zz, row : row + 128, par * 128 : par * 128 + 128]
                        up = v > 0
                        mean += jnp.where(up, v, leak_slope * v)
                        mask |= jnp.where(up, 1 << (zz * 4 + yy * 2 + par), 0)
            pooled[zp, yp] = (mean * 0.125).astype(jnp.bfloat16)
            lanes = slice(yp * 128, yp * 128 + 128)
            rows = pl.ds(pl.multiple_of(zp * 128, 128), 128)
            xt[6, rows, lanes] = mask.astype(jnp.float32).astype(jnp.bfloat16)


def first_section(vc, vzl, vzh, vyl, vyh, w1):
    return call(
        first_body,
        [
            ((2, 4, 128, 128), jnp.bfloat16),
            ((7, 256, 1280), jnp.bfloat16),
        ],
        [
            ((6, 1280, 256), jnp.bfloat16),
            ((2, 1024, 256), jnp.float32),
            ((256, 512), jnp.bfloat16),
        ],
        [vc, vzl, vzh, vyl, vyh, w1],
        flops=5_000_000_000,
        vmem=18,
        name="first",
    )


def lay_filters(place, tap_of, turn):
    for b in range(3):
        for four in range(4):
            for c in range(3):
                for two in range(2):
                    a = four - two
                    lanes = slice(c * 256 + two * 128, c * 256 + two * 128 + 128)
                    block = (b, slice(four * 128, four * 128 + 128), lanes)
                    if 0 <= a < 3:
                        tap = tap_of(a, b, c)
                        place[block] = tap.T if turn else tap
                    else:
                        place[block] = jnp.zeros((128, 128), jnp.bfloat16)


def conv_rows(source, lanes, filters, total, count):
    rows = count * 128
    parts = None
    for b in range(3):
        part = dot(source[b : b + count, :, lanes].reshape(rows, 512), filters[b])
        parts = part if parts is None else parts + part
    total[0:rows, :] = parts


def joined(total, y):
    rows = slice(y * 128, y * 128 + 128)
    return (
        row_before(total[rows, 0:256]) + total[rows, 256:512] + row_after(total[rows, 512:768])
    )


def cot_body(half, near, k3, core, hidden_grad, cot3, cells, filters, total):
    first = core[0] * 2
    for z in range(4):
        for y in range(8):
            lanes = pl.ds(pl.multiple_of((first + z) * 128, 128), 128)
            cells[y, :, lanes] = half[z, y].T
    for z in range(2):
        for y in range(8):
            lanes = pl.ds(pl.multiple_of((4 - 2 * first + z) * 128, 128), 128)
            cells[y, :, lanes] = near[z, y].T
    lay_filters(filters, lambda a, b, c: k3[(2 - a) * 9 + (2 - b) * 3 + 2 - c], True)
    for j in range(2):
        conv_rows(cells, slice(j * 256, j * 256 + 512), filters, total, 6)
        for y in range(6):
            hidden_grad[y, :, j * 256 : j * 256 + 256] = joined(total, y)
    for y in range(4):
        own = cells[y + 2, :, 256:512].astype(jnp.float32)
        rows = slice(y * 128, y * 128 + 128)
        cot3[rows, 0:256] = row_after(own).astype(jnp.bfloat16)
        cot3[rows, 256:512] = own.astype(jnp.bfloat16)
        cot3[rows, 512:768] = row_before(own).astype(jnp.bfloat16)


def cot_section(half, near, core, k3):
    return call(
        cot_body,
        [((6, 128, 512), jnp.float32), ((512, 768), jnp.bfloat16)],
        [
            ((8, 128, 768), jnp.bfloat16),
            ((3, 512, 768), jnp.bfloat16),
            ((768, 768), jnp.float32),
        ],
        [half, near, k3, core.reshape(1)],
        smem=1,
        flops=3_600_000_000,
        vmem=16,
        name="cot",
    )


def grad_taps(turned, cot3, store):
    for b in range(3):
        full = dot(turned[:, b * 128 : b * 128 + 512], cot3[...])
        for a in range(3):
            for c in range(3):
                low = full[a * 128 : a * 128 + 128, c * 256 : c * 256 + 128]
                high = full[a * 128 + 128 : a * 128 + 256, c * 256 + 128 : c * 256 + 256]
                store(9 * a + 3 * b + c, low + high)


def mid_body(
    own, near, far, ends, near_ends, far_ends, hidden_grad, cot3, k2, k3, flags, core,
    maps, spg, cells, hidden, filters, total, spg3, turned,
):
    at_near = 512 - 512 * core[0]
    for z in range(2):
        for part, part_ends, at in (
            (own, ends, None),
            (near, near_ends, at_near + z * 128),
            (far, far_ends, 512 - at_near + z * 128),
        ):
            lanes = (
                slice(256 + z * 128, 384 + z * 128)
                if at is None
                else pl.ds(pl.multiple_of(at, 128), 128)
            )
            for y in range(2):
                cells[y, :, lanes] = part_ends[z, y]
                cells[y + 6, :, lanes] = part_ends[z, y + 2]
            for y in range(4):
                cells[y + 2, :, lanes] = part[z, y]
    lay_filters(filters, lambda a, b, c: k2[9 * a + 3 * b + c], True)
    lane = lax.broadcasted_iota(jnp.int32, (128, 256), 1)
    for j in range(2):
        conv_rows(cells, slice(j * 256, j * 256 + 512), filters, total, 6)
        edge = lane < 128 if j == 0 else lane >= 128
        inside = jnp.where(edge, flags[j], 1.0)
        for y in range(6):
            pre = joined(total, y)
            keep = inside * flags[2] if y == 0 else inside * flags[3] if y == 5 else inside
            lanes = slice(j * 256, j * 256 + 256)
            up = pre > 0
            hidden[y, :, lanes] = (jnp.where(up, pre, leak_slope * pre) * keep).astype(
                jnp.bfloat16
            )
            back = hidden_grad[y, :, lanes]
            spg[y, :, lanes] = (jnp.where(up, back, leak_slope * back) * keep).astype(
                jnp.bfloat16
            )
    turned[...] = hidden[...].reshape(768, 512).T

    def store(place, value):
        for i in range(16):
            maps[(i + core[0]) % 2, i // 2, place] = value[i * 8 : i * 8 + 8]

    def store_third(tap, value):
        store(27 + tap, value)

    grad_taps(turned, cot3, store_third)
    store(54, jnp.zeros((128, 128), jnp.float32))
    store(55, jnp.zeros((128, 128), jnp.float32))
    for y in range(4):
        own = spg[y + 1, :, 128:384].astype(jnp.float32)
        rows = slice(y * 128, y * 128 + 128)
        spg3[rows, 0:256] = row_after(own).astype(jnp.bfloat16)
        spg3[rows, 256:512] = own.astype(jnp.bfloat16)
        spg3[rows, 512:768] = row_before(own).astype(jnp.bfloat16)
    turned[...] = cells[1:7, :, 128:640].reshape(768, 512).T

    def store_second(tap, value):
        store(tap, value.T)

    grad_taps(turned, spg3, store_second)
    lay_filters(filters, lambda a, b, c: k3[9 * a + 3 * b + c], False)
    conv_rows(hidden, slice(0, 512), filters, total, 4)
    for y in range(4):
        done = joined(total, y)
        for z in range(2):
            store(56 + z * 4 + y, done[:, z * 128 : z * 128 + 128].T)


def mid_section(
    own, near, far, ends, near_ends, far_ends, hidden_grad, cot3, k2, k3, flags, core
):
    return call(
        mid_body,
        [
            ((2, 8, 64, 8, 128), jnp.float32),
            ((6, 128, 512), jnp.bfloat16),
        ],
        [
            ((8, 128, 768), jnp.bfloat16),
            ((6, 128, 512), jnp.bfloat16),
            ((3, 512, 768), jnp.bfloat16),
            ((768, 768), jnp.float32),
            ((512, 768), jnp.bfloat16),
            ((512, 768), jnp.bfloat16),
        ],
        [own, near, far, ends, near_ends, far_ends, hidden_grad, cot3, k2, k3]
        + [flags, core.reshape(1)],
        smem=2,
        flops=7_000_000_000,
        vmem=26,
        name="mid",
    )


def last_body(spg, k2, xt, core, first, filters, total, back, full):
    lay_filters(filters, lambda a, b, c: k2[(2 - a) * 9 + (2 - b) * 3 + 2 - c], False)
    conv_rows(spg, slice(0, 512), filters, total, 4)
    for y in range(4):
        grad = joined(total, y).astype(jnp.bfloat16).astype(jnp.float32)
        for z in range(2):
            share = grad[:, z * 128 : z * 128 + 128] * 0.125
            up, down = share.astype(jnp.bfloat16), (share * leak_slope).astype(jnp.bfloat16)
            up, down = up.astype(jnp.float32), down.astype(jnp.float32)
            mask = xt[6, z * 128 : z * 128 + 128, y * 128 : y * 128 + 128]
            mask = mask.astype(jnp.float32).astype(jnp.int32)
            for zz in range(2):
                for yy in range(2):
                    for par in range(2):
                        bit = mask & (1 << (zz * 4 + yy * 2 + par))
                        row = (2 * y + yy) * 128
                        back[2 * z + zz, row : row + 128, par * 128 : par * 128 + 128] = (
                            jnp.where(bit != 0, up, down).astype(jnp.bfloat16)
                        )
    for b in range(3):
        parts = None
        for z in range(4):
            left = xt[z : z + 3, :, b * 128 : b * 128 + 1024].reshape(768, 1024)
            part = dot(left, back[z])
            parts = part if parts is None else parts + part
        full[...] = parts
        for a in range(3):
            for c in range(3):
                even, odd = ((2, 0), (0, 1), (1, 3))[c]
                low = full[a * 256 + even * 64 : a * 256 + even * 64 + 64, 0:128]
                high = full[a * 256 + odd * 64 : a * 256 + odd * 64 + 64, 128:256]
                tap = 9 * a + 3 * b + c
                row = tap // 4 * 128 + tap % 2 * 64
                first[(tap // 2 + core[0]) % 2, row : row + 64, :] = low + high
    first[core[0], 896:1024, :] = jnp.zeros((128, 128), jnp.float32)
    first[1 - core[0], 832:1024, :] = jnp.zeros((192, 128), jnp.float32)


def last_section(spg, k2, xt, core):
    return call(
        last_body,
        [((2, 1024, 128), jnp.float32)],
        [
            ((3, 512, 768), jnp.bfloat16),
            ((768, 768), jnp.float32),
            ((4, 1024, 256), jnp.bfloat16),
            ((768, 256), jnp.float32),
        ],
        [spg, k2, xt, core.reshape(1)],
        smem=1,
        flops=6_000_000_000,
        vmem=20,
        name="last",
    )[0]


def cot_rows(values):
    own = values.reshape(4, 8, 4, 8, 128)
    below = jnp.pad(own[:, :7, 2:], ((0, 0), (1, 0), (0, 0), (0, 0), (0, 0)))
    above = jnp.pad(own[:, 1:, :2], ((0, 0), (0, 1), (0, 0), (0, 0), (0, 0)))
    return jnp.swapaxes(jnp.concatenate([below, own, above], axis=2), 0, 1)


def cot_deep(values):
    own = values.reshape(8, 4, 8, 8, 128)
    ends = ((0, 0),) * 4
    below = jnp.pad(own[:7, 2:], ((1, 0),) + ends)
    above = jnp.pad(own[1:, :2], ((0, 1),) + ends)
    return jnp.concatenate([below, own, above], axis=1).reshape(16, 4, 8, 8, 128)


def after(values, *done):
    return lax.optimization_barrier((values,) + done)[0]


def on_device(volume, first_kernel, second_kernel, third_kernel, cotangent):
    sx, sy = lax.axis_index("sx"), lax.axis_index("sy")
    core = sx % 2
    flags = jnp.stack([sx > 0, sx < 15, sy > 0, sy < 7]).astype(jnp.float32)
    shares = jnp.concatenate(
        [jnp.swapaxes(second_kernel, 3, 4).reshape(216, 128), third_kernel.reshape(216, 128)]
    )
    filters = lax.all_gather(shares, "sx", axis=0, tiled=True)
    vc = jnp.swapaxes(volume, 2, 3)
    near, far = partners(vc[:1], vc[-1:], shares)
    vzl, vzh = jnp.where(core == 0, far, near), jnp.where(core == 0, near, far)
    deep = lambda y: jnp.concatenate([vzl[:, y : y + 1], vc[:, y : y + 1], vzh[:, y : y + 1]])
    vyl, vyh = neighbours(deep(0), deep(7), "sy")
    cot_tall = to_sy(after(cot_rows(jnp.swapaxes(cotangent, 2, 3)), near))
    cot_parts = lax.all_to_all(cot_deep(cot_tall), "sx", 0, 0, tiled=True)
    cot_half = cot_parts.transpose(1, 2, 0, 3, 4).reshape(4, 8, 128, 128)
    cot_half = lax.optimization_barrier(cot_half)
    cot_near = other_core(jnp.where(core == 0, cot_half[2:], cot_half[:2]))
    w1 = after(pair_filters(first_kernel), cot_tall)
    pooled, xt = first_section(vc, vzl, vzh, vyl, vyh, w1)
    pyl, pyh = neighbours(pooled[:, :2], pooled[:, 2:], "sy")
    near, far = partners(pooled, pooled)
    ends = jnp.concatenate([pyl, pyh], axis=1)
    near_ends, far_ends = partners(ends, ends)
    filters = filters.reshape(16, 54, 8, 128).swapaxes(0, 1).reshape(54, 128, 128)
    k2, k3 = filters[:27], filters[27:]
    hidden_grad, cot3 = cot_section(cot_half, cot_near, core, k3)
    maps, spg = mid_section(
        pooled, near, far, ends, near_ends, far_ends, hidden_grad, cot3, k2, k3, flags, core
    )
    from_other = other_core(maps[1].astype(jnp.bfloat16))
    own = maps[0]
    mine, theirs = own[:, 56:].astype(jnp.bfloat16), from_other[:, 56:]
    first_part = last_section(spg, k2, xt, core)
    first_from = other_core(first_part[1].astype(jnp.bfloat16))
    first_half = first_part[0] + first_from.astype(jnp.float32)
    grads = own[:, :56] + from_other[:, :56].astype(jnp.float32)
    parts = jnp.concatenate(
        [
            grads.astype(jnp.bfloat16),
            jnp.where(core == 0, mine, theirs),
            jnp.where(core == 0, theirs, mine),
            first_half.astype(jnp.bfloat16).reshape(8, 16, 8, 128),
        ],
        axis=1,
    )
    parts = to_chips(parts)
    parts = jnp.concatenate(
        [
            sum_first(parts[:, :56]).astype(jnp.bfloat16).reshape(8, 7, 8, 128),
            sum_first(parts[:, 72:]).astype(jnp.bfloat16).reshape(8, 2, 8, 128),
            parts[:, 56:72],
        ],
        axis=1,
    )
    parts = to_sy(parts)
    output = parts[:, 9:].reshape(8, 4, 4, 8, 128).swapaxes(0, 1).reshape(4, 32, 8, 128)
    share = to_sy(repeated(sum_first(parts[:, :9]).astype(jnp.bfloat16), 8))
    grads = share[:, :7].reshape(56, 8, 128)[:54].astype(jnp.float32)
    grads = grads.reshape(2, 3, 3, 3, 8, 128)
    first_grad = repeated(share[:, 7:].reshape(128, 128), 16)
    first_grad = lax.all_to_all(first_grad, "sx", 0, 0, tiled=True).reshape(2048, 128)[:1728]
    first_grad = first_grad.astype(jnp.float32).reshape(3, 3, 3, 64, 128)
    return (jnp.swapaxes(output, 2, 3), first_grad, jnp.swapaxes(grads[0], 3, 4), grads[1])


def solution(mesh):
    in_specs = (
        P("sx", "sy", None, None),
        P(),
        P(None, None, None, None, "sx"),
        P(None, None, None, "sx", None),
        P("sy", None, None, "sx"),
    )
    out_specs = (
        P("sy", None, None, "sx"),
        P(),
        P(None, None, None, None, "sx"),
        P(None, None, None, "sx", None),
    )
    return jax.shard_map(
        on_device, mesh=mesh, in_specs=in_specs, out_specs=out_specs, check_vma=False
    )
```
